512 devices in a mesh: view: 16 (over y, z_hi), space: 32 (over x, z_lo, core).
Axes of the slice: x: 4, y: 4, z: 16 (z_hi: 4, z_lo: 4; z = z_hi * 4 + z_lo), core: 2. Of those that a mesh axis runs over, the one named last changes fastest.
Arguments:
- latent: bfloat16 [64, 8, 32, 128], P('view', None, 'space'), may hold values from -12 to 12
- camera_edges: int32 [96, 2], replicated, may hold values from 0 to 63, as said below
- conv_in_weight: bfloat16 [3, 3, 8, 1024], replicated, may hold values from -0.75 to 0.75
- query_weight: bfloat16 [1024, 512], replicated, may hold values from -8.75 to 8.75
- key_value_weight: bfloat16 [1024, 1024], replicated, may hold values from -0.1875 to 0.1875
- out_weight: bfloat16 [512, 1024], replicated, may hold values from -0.25 to 0.25
- conv_out_weight: bfloat16 [3, 3, 8, 1024], replicated, may hold values from -0.0625 to 0.0625
Outputs:
- prediction: float32 [64, 8, 32, 128], P('view', None, 'space')
The draws below stay inside these ranges and needn't reach their ends.
Inputs may be any that keep to these rules, and one draw needn't show every extreme that they name: `camera_edges`: each row is a pair (a, b) with b = (a + d) mod 64 for some d from 1 to 2; no pair appears twice.
All inputs are finite; a program needn't handle non-finite values.
Results may differ from the reference program's by a relative error of at most 0.028.
Values may be sent and summed in bfloat16 or wider, within the bound.
No kernel may reach another device: no remote copies, remote signals or barrier semaphores. Data moves between devices by JAX's collectives and lax.ppermute only.
A program may use at most 64 MiB of HBM per device.

```python
import math
import jax
import jax.numpy as jnp
from jax import lax

D = 1024
HEADS = 8
HD = 64
LC = 8
W = 128
REACH = 2
R = 1
VIEWS = 64
H = 32
EDGES = 96


def draw_latent(key, part):
    key = jax.random.fold_in(key, 11)
    entry_key, spread_key = jax.random.split(key)
    entries = jax.random.truncated_normal(entry_key, -4.0, 4.0, (VIEWS, LC, H, W), jnp.float32)
    spread = jax.random.uniform(spread_key, (VIEWS, 1, H, W), jnp.float32, jnp.log(0.3), jnp.log(3.0))
    return (entries * jnp.exp(spread)).astype(jnp.bfloat16)


def draw_query_weight(key, part):
    key = jax.random.fold_in(key, 23)
    entry_key = jax.random.fold_in(key, 0)
    unit_size = 4.0 / D ** 0.5
    entries = jax.random.truncated_normal(entry_key, -4.0, 4.0, (D, HEADS * HD), jnp.float32)
    return (entries * unit_size).astype(jnp.bfloat16)


def draw_camera_edges(key, part):
    key = jax.random.fold_in(key, 37)
    pair_count = VIEWS * REACH
    ranking = jax.random.permutation(key, pair_count).astype(jnp.int32)
    ranking = ranking.at[pair_count - 1].set(pair_count)
    ranking = ranking.at[pair_count - REACH].set(pair_count + 1)
    chosen = lax_top(ranking)
    source = chosen // REACH
    target = (source + chosen % REACH + 1) % VIEWS
    return jnp.stack([source, target], axis=1).astype(jnp.int32)


def lax_top(ranking):
    return jax.lax.top_k(ranking, EDGES)[1].astype(jnp.int32)


def normal_values(stream_key, shape, scale, most, kind=jnp.bfloat16):
    return jnp.clip(scale * jax.random.normal(stream_key, shape, jnp.float32), -most, most).astype(kind)


def setup_inputs(seed: int = 0) -> dict:
    splits = jax.random.split(jax.random.key(seed), 8)
    latent = draw_latent(jax.random.fold_in(splits[7], 71), 0)
    camera_edges = draw_camera_edges(jax.random.fold_in(splits[7], 71), 0)
    conv_in_weight = normal_values(splits[2], (3, 3, LC, D), (9 * LC) ** -0.5, 0.75)
    query_weight = draw_query_weight(jax.random.fold_in(splits[7], 71), 0)
    key_value_weight = normal_values(splits[4], (D, 2 * HEADS * HD), D ** -0.5, 0.1875)
    out_weight = normal_values(splits[5], (HEADS * HD, D), (HEADS * HD) ** -0.5, 0.25)
    conv_out_weight = normal_values(splits[6], (3, 3, LC, D), (9 * D) ** -0.5, 0.0625)
    return {"latent": latent, "camera_edges": camera_edges, "conv_in_weight": conv_in_weight, "query_weight": query_weight, "key_value_weight": key_value_weight, "out_weight": out_weight, "conv_out_weight": conv_out_weight}


NEG_FILL = -1e+30

def conv_in_apply(framed, weight, row_count):
    padded = jnp.pad(framed, ((0, 0), (0, 0), (0, 0), (1, 1)))
    columns = framed.shape[3]
    pieces = [padded[:, :, i:i + row_count, j:j + columns] for i in range(3) for j in range(3)]
    stacked = jnp.stack(pieces, axis=1)
    patches = jnp.transpose(stacked, (0, 3, 4, 1, 2)).reshape(framed.shape[0], row_count, columns, 9 * framed.shape[1])
    flattened = weight.reshape(9 * weight.shape[2], weight.shape[3])
    return jnp.dot(patches, flattened, preferred_element_type=jnp.float32).astype(jnp.bfloat16)

def normalize(hidden):
    widened = hidden.astype(jnp.float32)
    scaling = lax.rsqrt(lax.optimization_barrier(jnp.mean(widened * widened, axis=-1, keepdims=True)) + 1e-06)
    return (widened * scaling).astype(jnp.bfloat16)

def conv_out_view(padded, weight):
    row_count = padded.shape[0] - 2
    columns = padded.shape[1] - 2
    summed = jnp.zeros((weight.shape[2], row_count, columns), jnp.float32)
    for i in range(3):
        for j in range(3):
            window = padded[i:i + row_count, j:j + columns].astype(jnp.float32)
            summed = summed + jnp.einsum('rwd,cd->crw', window, weight[i, j].astype(jnp.float32))
    return summed

def reference(latent, camera_edges, conv_in_weight, query_weight, key_value_weight, out_weight, conv_out_weight):
    framed = jnp.pad(latent, ((0, 0), (0, 0), (1, 1), (0, 0)))

    def front(view_rows):
        hidden = conv_in_apply(view_rows[None], conv_in_weight, H)[0]
        normed = normalize(hidden)
        queries = jnp.dot(normed, query_weight, preferred_element_type=jnp.float32).astype(jnp.bfloat16)
        key_values = jnp.dot(normed, key_value_weight, preferred_element_type=jnp.float32).astype(jnp.bfloat16)
        return (hidden, queries, key_values)
    hidden, queries, key_values = lax.map(front, framed)
    view_ids = jnp.arange(VIEWS, dtype=jnp.int32)
    source = camera_edges[:, 0][:, None, None]
    target = camera_edges[:, 1][:, None, None]
    linked = jnp.any((source == view_ids[None, :, None]) & (target == view_ids[None, None, :]) | (target == view_ids[None, :, None]) & (source == view_ids[None, None, :]), axis=0)
    offsets = jnp.arange(-REACH, REACH + 1, dtype=jnp.int32)
    band_count = H // R
    scaling = 1.0 / math.sqrt(HD)

    def mix(view):
        other_views = (view + offsets) % VIEWS
        link_row = lax.dynamic_index_in_dim(linked, view, 0, False)
        allowed = jnp.take(link_row, other_views) | (offsets == 0)
        nearby = jnp.take(key_values, other_views, axis=0).reshape(2 * REACH + 1, band_count, R * W, 2, HEADS, HD)
        asked = lax.dynamic_index_in_dim(queries, view, 0, False).reshape(band_count, R * W, HEADS, HD).astype(jnp.float32)
        near_keys = nearby[:, :, :, 0].astype(jnp.float32)
        near_values = nearby[:, :, :, 1].astype(jnp.float32)
        scores = jnp.einsum('bthe,obshe->bhtos', asked, near_keys) * scaling
        scores = jnp.where(allowed[None, None, None, :, None], scores, NEG_FILL)
        largest = lax.optimization_barrier(jnp.max(scores, axis=(3, 4), keepdims=True))
        raised = jnp.exp(scores - largest)
        summed = lax.optimization_barrier(jnp.sum(raised, axis=(3, 4), keepdims=True))
        soft_weights = lax.optimization_barrier((raised / summed).astype(jnp.bfloat16)).astype(jnp.float32)
        attended = jnp.einsum('bhtos,obshe->bthe', soft_weights, near_values).astype(jnp.bfloat16)
        attended = attended.reshape(H, W, HEADS * HD)
        branch = jnp.dot(attended, out_weight, preferred_element_type=jnp.float32)
        own_hidden = lax.dynamic_index_in_dim(hidden, view, 0, False)
        return (own_hidden.astype(jnp.float32) + branch).astype(jnp.bfloat16)
    hidden_next = lax.map(mix, view_ids)
    padded = jnp.pad(hidden_next, ((0, 0), (1, 1), (1, 1), (0, 0)))
    return lax.map(lambda single: conv_out_view(single, conv_out_weight), padded)
```

```python
import functools
import math

import jax
import jax.numpy as jnp
from jax import lax
from jax.experimental import pallas as pl
from jax.experimental.pallas import tpu as pltpu
from jax.sharding import PartitionSpec as P

HEADS = 8
HD = 64
REACH = 2
TAPS = 72
DEEP = 256
NEG_FILL = -1e30
MIB = 1024 * 1024


def nt_dot(a, b, precision=None):
    return lax.dot_general(
        a, b, (((1,), (1,)), ((), ())), preferred_element_type=jnp.float32, precision=precision
    )


def high(x):
    return x.astype(jnp.bfloat16).astype(jnp.float32)


def split_lanes(x):
    lane = lax.broadcasted_iota(jnp.int32, x.shape, 1)
    first = high(x)
    rest = x - first
    second = high(rest)
    third = rest - second
    return jnp.where(lane < TAPS, first, jnp.where(lane < 2 * TAPS, second, third)).astype(
        jnp.bfloat16
    )


def flat_taps(ref):
    rows = [ref[i, j].astype(jnp.float32) for i in range(3) for j in range(3)]
    return jnp.concatenate(rows, axis=0)


def prepare_kernel(
    views, edges_hbm, conv_in_hbm, wq_hbm, wkv_hbm, wo_hbm, conv_out_hbm,
    gc, mq, mkv, nt, bias, edges_ref, conv_in, wq, wkv, wo, conv_out, sems,
):
    copies = [
        pltpu.make_async_copy(src, dst, sems.at[n])
        for n, (src, dst) in enumerate(
            (
                (edges_hbm, edges_ref),
                (conv_in_hbm, conv_in),
                (conv_out_hbm, conv_out),
                (wq_hbm, wq),
                (wkv_hbm, wkv),
                (wo_hbm, wo),
            )
        )
    ]
    for copy in copies:
        copy.start()
    local = bias.shape[0]
    span = bias.shape[1]
    total = views * local
    first = lax.axis_index("view") * local
    copies[0].wait()
    source = edges_ref[0:1, :]
    target = edges_ref[1:2, :]
    slot = lax.broadcasted_iota(jnp.int32, (span, 1), 0)
    near = first - REACH + slot
    near = jnp.where(near < 0, near + total, near)
    near = jnp.where(near >= total, near - total, near)
    for v in range(local):
        own = first + v
        hit = ((source == own) & (target == near)) | ((target == own) & (source == near))
        linked = jnp.max(hit.astype(jnp.float32), axis=1, keepdims=True)
        linked = jnp.where(slot == v + REACH, 1.0, linked)
        inside = (slot >= v) & (slot <= v + 2 * REACH)
        allowed = (linked > 0.5) & inside
        bias[v] = jnp.broadcast_to(jnp.where(allowed, 0.0, NEG_FILL), bias.shape[1:])
    copies[1].wait()
    wc = flat_taps(conv_in)
    wcb = wc.astype(jnp.bfloat16)
    copies[2].wait()
    wt = flat_taps(conv_out)
    pad = jnp.zeros((DEEP - 3 * TAPS, wc.shape[1]), jnp.float32)
    wc3 = jnp.concatenate([wc, wc, wc, pad], axis=0).astype(jnp.bfloat16)
    both = jnp.concatenate([wc, wt], axis=0).astype(jnp.bfloat16)
    wtb = wt.astype(jnp.bfloat16)
    gc[...] = split_lanes(nt_dot(both, wc3))
    copies[3].wait()
    mq[...] = jnp.dot(wcb, wq[...], preferred_element_type=jnp.float32)
    copies[4].wait()
    mkv[...] = jnp.dot(wcb, wkv[...], preferred_element_type=jnp.float32)
    copies[5].wait()
    nt[...] = nt_dot(wtb, wo[...])


def head_products(mq_ref, mkv_ref, nt_ref, aq, bb):
    lane = lax.broadcasted_iota(jnp.int32, (TAPS, 2 * HD), 1)
    even = (lane < HD).astype(jnp.float32)
    odd = 1.0 - even
    hpad = jnp.zeros((DEEP - 3 * TAPS, 2 * HD), jnp.float32)
    scale = math.log2(math.e) / math.sqrt(HD)
    for g in range(HEADS // 2):
        cols = slice(g * 2 * HD, (g + 1) * 2 * HD)
        vcols = slice(HEADS * HD + g * 2 * HD, HEADS * HD + (g + 1) * 2 * HD)
        q = mq_ref[:, cols] * scale
        k = mkv_ref[:, cols]
        v = mkv_ref[:, vcols]
        q3 = jnp.concatenate([q, q, q, hpad], axis=0)
        k2 = jnp.concatenate([k * even, k * odd], axis=0)
        v2 = jnp.concatenate([v * even, v * odd], axis=0)
        aq[(g + 1) * 2 * TAPS : (g + 2) * 2 * TAPS, :] = split_lanes(
            nt_dot(k2, q3, lax.Precision.HIGHEST)
        )
        b = nt_dot(nt_ref[:, cols], v2, lax.Precision.HIGHEST)
        bh = high(b)
        bb[g] = jnp.concatenate([bh, b - bh], axis=0).astype(jnp.bfloat16)


def shifted(x, by):
    lane = lax.broadcasted_iota(jnp.int32, x.shape, x.ndim - 1)
    width = x.shape[-1]
    if by == 1:
        return jnp.where(lane == 0, 0.0, pltpu.roll(x, 1, x.ndim - 1))
    return jnp.where(lane == width - 1, 0.0, pltpu.roll(x, width - 1, x.ndim - 1))


def is_even(axis):
    return lax.rem(lax.axis_index(axis), 2) == 0


def pack_kernel(own, first, second, after, rows, late, early):
    local = own.shape[0]
    even = is_even("space")
    kind = own.dtype
    for v in range(local):
        one = first[v].astype(jnp.float32)
        two = second[v].astype(jnp.float32)
        rows[v, 0] = jnp.where(even, two, one).astype(kind)
        rows[v, 1] = own[v]
        rows[v, 2] = jnp.where(even, one, two).astype(kind)
    even = is_even("view")
    for n in range(REACH):
        for i in range(3):
            tail = rows[local - REACH + n, i].astype(jnp.float32)
            lead = rows[n, i].astype(jnp.float32)
            early[n, i] = jnp.where(even, tail, lead).astype(kind)
            late[n, i] = jnp.where(even, lead, tail).astype(kind)


def patch_stack(rows):
    parts = []
    for row in rows:
        row = row.astype(jnp.float32)
        parts += [shifted(row, 1), row, shifted(row, -1)]
    patch = jnp.concatenate(parts, axis=0)
    pad = jnp.zeros((DEEP - 3 * TAPS, patch.shape[1]), jnp.float32)
    return jnp.concatenate([patch, patch, patch, pad], axis=0).astype(jnp.bfloat16)


def token_rate(gram_patches, patches):
    square = jnp.sum(gram_patches * patches, axis=0, keepdims=True) * (1.0 / 1024)
    return lax.rsqrt(jnp.maximum(square, 0.0) + 1e-6)


def store_keys(keyed, slots, ahead, kl, vl):
    w = keyed.shape[1] // len(slots)
    kh = high(keyed)
    low = keyed - kh
    sub = lax.broadcasted_iota(jnp.int32, (8, w), 0)
    for n, u in enumerate(slots):
        cols = slice(n * w, (n + 1) * w)
        place = slice(u * w, (u + 1) * w)
        onehot = (sub == u + ahead).astype(jnp.float32)
        h = kh[:, cols]
        r = low[:, cols]
        vl[:, place] = jnp.concatenate([h, jnp.ones((8, w), jnp.float32), r], axis=0).astype(
            jnp.bfloat16
        )
        tall = jnp.concatenate(
            [h, onehot, r, h, jnp.zeros((DEEP - 3 * TAPS - 8, w), jnp.float32)], axis=0
        )
        kl[place, :] = tall.T.astype(jnp.bfloat16)


def own_kernel(rows, gc, mq, mkv, nt, bias, qr, skip, kl, vl, bb, p3, aq):
    local, _, _, w = rows.shape
    aq[0 : 2 * TAPS, :] = gc[...]
    head_products(mq, mkv, nt, aq, bb)
    for v in range(local):
        p3[:, v * w : (v + 1) * w] = patch_stack([rows[v, i] for i in range(3)])
    asked = jnp.dot(aq[...], p3[...], preferred_element_type=jnp.float32)
    patches = p3[0:TAPS, :].astype(jnp.float32)
    rate = token_rate(asked[0:TAPS], patches)
    skip[...] = asked[TAPS : 2 * TAPS]
    store_keys(patches * rate, range(local), REACH, kl, vl)
    for v in range(local):
        for head in range(HEADS):
            q = asked[(head + 2) * TAPS : (head + 3) * TAPS, v * w : (v + 1) * w]
            q = q * rate[:, v * w : (v + 1) * w]
            h = high(q)
            qr[v, :, head * w : (head + 1) * w] = jnp.concatenate(
                [h, bias[v], h, q - h, jnp.zeros((DEEP - 3 * TAPS - 8, w), jnp.float32)], axis=0
            ).astype(jnp.bfloat16)


def mix_kernel(
    second, first, gc, bb, qr, skip, own_kl, own_vl,
    mine, late, early, p3, kl, vl, uh, ul, sc, ex,
):
    local, _, w = mine.shape
    even = is_even("view")
    for u in range(REACH):
        one = [first[u, i].astype(jnp.float32) for i in range(3)]
        two = [second[u, i].astype(jnp.float32) for i in range(3)]
        prev = [jnp.where(even, b, a) for a, b in zip(one, two)]
        nxt = [jnp.where(even, a, b) for a, b in zip(one, two)]
        p3[:, u * w : (u + 1) * w] = patch_stack(prev)
        p3[:, (REACH + u) * w : (REACH + u + 1) * w] = patch_stack(nxt)
    gram = jnp.dot(gc[0:TAPS, :], p3[...], preferred_element_type=jnp.float32)
    patches = p3[0:TAPS, :].astype(jnp.float32)
    rate = token_rate(gram, patches)
    slots = [*range(REACH), *range(REACH + local, 2 * REACH + local)]
    store_keys(patches * rate, slots, 0, kl, vl)
    inner = slice(REACH * w, (REACH + local) * w)
    kl[inner, :] = own_kl[...]
    vl[:, inner] = own_vl[...]
    reach = (2 * REACH + 1) * w
    sc[0] = jnp.dot(kl[0:reach, :], qr[0], preferred_element_type=jnp.float32)
    for v in range(local):
        if v + 1 < local:
            sc[(v + 1) % 2] = jnp.dot(
                kl[(v + 1) * w : (v + 1) * w + reach, :], qr[v + 1],
                preferred_element_type=jnp.float32,
            )
        for head in range(HEADS):
            cols = slice(head * w, (head + 1) * w)
            scores = sc[v % 2, :, cols]
            largest = jnp.max(scores, axis=0, keepdims=True)
            ex[v % 2, :, cols] = jnp.exp2(scores - largest).astype(jnp.bfloat16)
        gathered = jnp.dot(
            vl[:, v * w : v * w + reach], ex[v % 2], preferred_element_type=jnp.float32
        )
        mixed = (gathered[0:TAPS] + gathered[TAPS + 8 :]) / gathered[TAPS : TAPS + 1]
        for g in range(HEADS // 2):
            pair = mixed[:, g * 2 * w : (g + 1) * 2 * w]
            pair = jnp.concatenate([pair[:, :w], pair[:, w:]], axis=0)
            h = pair.astype(jnp.bfloat16)
            uh[g, :, v * w : (v + 1) * w] = h
            ul[g, :, v * w : (v + 1) * w] = (pair - h.astype(jnp.float32)).astype(jnp.bfloat16)
    z = skip[...]
    for g in range(HEADS // 2):
        y = jnp.dot(bb[g], uh[g], preferred_element_type=jnp.float32)
        z = z + y[:TAPS] + y[TAPS:]
        z = z + jnp.dot(bb[g, 0:TAPS, :], ul[g], preferred_element_type=jnp.float32)
    even = is_even("space")
    for v in range(local):
        parts = []
        for i in range(3):
            rows = z[i * 24 : (i + 1) * 24, v * w : (v + 1) * w]
            parts.append(shifted(rows[0:8], 1) + rows[8:16] + shifted(rows[16:24], -1))
        below, mine[v], above = parts
        early[v] = jnp.where(even, below, above)
        late[v] = jnp.where(even, above, below)


def pairs(count, start, closed):
    ends = count if closed else count - 1
    both = []
    for i in range(start, ends, 2):
        both += [(i, (i + 1) % count), ((i + 1) % count, i)]
    return both


def on_device(
    latent,
    camera_edges,
    conv_in_weight,
    query_weight,
    key_value_weight,
    out_weight,
    conv_out_weight,
):
    local, channels, _, w = latent.shape
    span = local + 2 * REACH
    views = lax.axis_size("view")
    space = lax.axis_size("space")
    x = latent.reshape(local, channels, w)
    row_first = lax.ppermute(x, "space", pairs(space, 0, False))
    row_second = lax.ppermute(x, "space", pairs(space, 1, False))

    f32, bf16 = jnp.float32, jnp.bfloat16
    whole = pl.BlockSpec(memory_space=pltpu.VMEM)
    far = pl.BlockSpec(memory_space=pltpu.HBM)
    loaded = (
        camera_edges.T,
        conv_in_weight,
        query_weight,
        key_value_weight,
        out_weight,
        conv_out_weight,
    )
    gc, mq, mkv, nt, bias = pl.pallas_call(
        functools.partial(prepare_kernel, views),
        in_specs=[far] * len(loaded),
        out_specs=[whole] * 5,
        out_shape=[
            pltpu.VMEM((2 * TAPS, DEEP), bf16),
            pltpu.VMEM((TAPS, HEADS * HD), f32),
            pltpu.VMEM((TAPS, 2 * HEADS * HD), f32),
            pltpu.VMEM((TAPS, HEADS * HD), f32),
            pltpu.VMEM((local, span, w), f32),
        ],
        scratch_shapes=[pltpu.VMEM(a.shape, a.dtype) for a in loaded]
        + [pltpu.SemaphoreType.DMA((len(loaded),))],
        compiler_params=pltpu.CompilerParams(vmem_limit_bytes=60 * MIB),
        cost_estimate=pl.CostEstimate(
            flops=3_000_000_000, bytes_accessed=5_000_000, transcendentals=0
        ),
    )(*loaded)

    part = jax.ShapeDtypeStruct((REACH, 3, channels, w), bf16)
    rows, late, early = pl.pallas_call(
        pack_kernel,
        in_specs=[whole] * 3 + [pl.BlockSpec(memory_space=pl.ANY)],
        out_specs=[whole] * 3,
        out_shape=[jax.ShapeDtypeStruct((local, 3, channels, w), bf16), part, part],
        compiler_params=pltpu.CompilerParams(vmem_limit_bytes=4 * MIB),
    )(x, row_first, row_second, bias)
    view_second = lax.ppermute(late, "view", pairs(views, 1, True))
    view_first = lax.ppermute(early, "view", pairs(views, 0, True))

    qr, skip, own_kl, own_vl, bb = pl.pallas_call(
        own_kernel,
        in_specs=[whole] * 6,
        out_specs=[whole] * 5,
        out_shape=[
            jax.ShapeDtypeStruct((local, DEEP, HEADS * w), bf16),
            jax.ShapeDtypeStruct((TAPS, local * w), f32),
            jax.ShapeDtypeStruct((local * w, DEEP), bf16),
            jax.ShapeDtypeStruct((2 * TAPS + 8, local * w), bf16),
            jax.ShapeDtypeStruct((HEADS // 2, 2 * TAPS, 2 * TAPS), bf16),
        ],
        scratch_shapes=[
            pltpu.VMEM((DEEP, local * w), bf16),
            pltpu.VMEM(((HEADS + 2) * TAPS, DEEP), bf16),
        ],
        compiler_params=pltpu.CompilerParams(vmem_limit_bytes=24 * MIB),
        cost_estimate=pl.CostEstimate(
            flops=3_000_000_000, bytes_accessed=1_000_000, transcendentals=0
        ),
    )(rows, gc, mq, mkv, nt, bias)

    plane = jax.ShapeDtypeStruct((local, channels, w), f32)
    mine, late, early = pl.pallas_call(
        mix_kernel,
        in_specs=[whole] * 8,
        out_specs=[whole] * 3,
        out_shape=[plane] * 3,
        scratch_shapes=[
            pltpu.VMEM((DEEP, 2 * REACH * w), bf16),
            pltpu.VMEM((span * w, DEEP), bf16),
            pltpu.VMEM((2 * TAPS + 8, span * w), bf16),
        ]
        + [pltpu.VMEM((HEADS // 2, 2 * TAPS, local * w), bf16)] * 2
        + [
            pltpu.VMEM((2, (2 * REACH + 1) * w, HEADS * w), f32),
            pltpu.VMEM((2, (2 * REACH + 1) * w, HEADS * w), bf16),
        ],
        compiler_params=pltpu.CompilerParams(vmem_limit_bytes=24 * MIB),
        cost_estimate=pl.CostEstimate(
            flops=6_000_000_000, bytes_accessed=1_000_000, transcendentals=3_000_000
        ),
    )(view_second, view_first, gc, bb, qr, skip, own_kl, own_vl)

    row_second = lax.ppermute(late, "space", pairs(space, 1, False))
    row_first = lax.ppermute(early, "space", pairs(space, 0, False))
    return (row_second + mine + row_first).reshape(local, channels, 1, w)


def solution(mesh):
    placed = (P("view", None, "space", None), P(), P(), P(), P(), P(), P())
    return jax.shard_map(
        on_device,
        mesh=mesh,
        in_specs=placed,
        out_specs=P("view", None, "space", None),
        check_vma=False,
    )
```

```python
import functools
import math

import jax
import jax.numpy as jnp
from jax import lax
from jax.experimental import pallas as pl
from jax.experimental.pallas import tpu as pltpu
from jax.sharding import PartitionSpec as P

HEADS = 8
HD = 64
REACH = 2
TAPS = 72
DEEP = 256
NEG_FILL = -1e30
MIB = 1024 * 1024


def nt_dot(a, b):
    return lax.dot_general(a, b, (((1,), (1,)), ((), ())), preferred_element_type=jnp.float32)


def high(x):
    return x.astype(jnp.bfloat16).astype(jnp.float32)


def split_lanes(x):
    lane = lax.broadcasted_iota(jnp.int32, x.shape, 1)
    first = high(x)
    rest = x - first
    second = high(rest)
    third = rest - second
    return jnp.where(lane < TAPS, first, jnp.where(lane < 2 * TAPS, second, third)).astype(
        jnp.bfloat16
    )


def flat_taps(ref):
    rows = [ref[i, j].astype(jnp.float32) for i in range(3) for j in range(3)]
    return jnp.concatenate(rows, axis=0)


def prepare_kernel(
    views, edges_hbm, conv_in_hbm, conv_out_hbm, wq_hbm, wkv_hbm, wo_hbm,
    gc, mq, mkv, nt, bias, edges_ref, conv_in, conv_out, wq, wk, wv, wo, sems,
):
    wide = HEADS * HD
    keys, values = slice(0, wide), slice(wide, 2 * wide)
    parts = (
        (edges_hbm, edges_ref),
        (conv_in_hbm, conv_in),
        (wq_hbm, wq),
        (wkv_hbm.at[:, keys], wk),
        (conv_out_hbm, conv_out),
        (wkv_hbm.at[:, values], wv),
        (wo_hbm, wo),
    )
    copies = [pltpu.make_async_copy(src, dst, sems.at[n]) for n, (src, dst) in enumerate(parts)]
    for copy in copies[:4]:
        copy.start()
    local = bias.shape[0]
    span = bias.shape[1]
    total = views * local
    first = lax.axis_index("view") * local
    copies[0].wait()
    source = edges_ref[0:1, :]
    target = edges_ref[1:2, :]
    slot = lax.broadcasted_iota(jnp.int32, (span, 1), 0)
    near = first - REACH + slot
    near = jnp.where(near < 0, near + total, near)
    near = jnp.where(near >= total, near - total, near)
    for v in range(local):
        own = first + v
        hit = ((source == own) & (target == near)) | ((target == own) & (source == near))
        linked = jnp.max(hit.astype(jnp.float32), axis=1, keepdims=True)
        linked = jnp.where(slot == v + REACH, 1.0, linked)
        inside = (slot >= v) & (slot <= v + 2 * REACH)
        allowed = (linked > 0.5) & inside
        bias[v] = jnp.broadcast_to(jnp.where(allowed, 0.0, NEG_FILL), bias.shape[1:])
    copies[1].wait()
    copies[4].start()
    wc = flat_taps(conv_in)
    wcb = wc.astype(jnp.bfloat16)
    copies[2].wait()
    copies[5].start()
    mq[...] = jnp.dot(wcb, wq[...], preferred_element_type=jnp.float32)
    copies[3].wait()
    copies[6].start()
    mkv[:, keys] = jnp.dot(wcb, wk[...], preferred_element_type=jnp.float32)
    copies[4].wait()
    wt = flat_taps(conv_out)
    pad = jnp.zeros((DEEP - 3 * TAPS, wc.shape[1]), jnp.float32)
    wc3 = jnp.concatenate([wc, wc, wc, pad], axis=0).astype(jnp.bfloat16)
    both = jnp.concatenate([wc, wt], axis=0).astype(jnp.bfloat16)
    gc[...] = split_lanes(nt_dot(both, wc3))
    copies[5].wait()
    mkv[:, values] = jnp.dot(wcb, wv[...], preferred_element_type=jnp.float32)
    copies[6].wait()
    nt[...] = nt_dot(wt.astype(jnp.bfloat16), wo[...])


def nt_dot_parts(a, b):
    ah, bh = high(a), high(b)
    left = jnp.concatenate([ah, a - ah, ah], axis=1).astype(jnp.bfloat16)
    right = jnp.concatenate([bh, bh, b - bh], axis=1).astype(jnp.bfloat16)
    return nt_dot(left, right)


def head_products(mq_ref, mkv_ref, nt_ref, aq, bb):
    lane = lax.broadcasted_iota(jnp.int32, (TAPS, 2 * HD), 1)
    even = (lane < HD).astype(jnp.float32)
    odd = 1.0 - even
    hpad = jnp.zeros((DEEP - 3 * TAPS, 2 * HD), jnp.float32)
    scale = math.log2(math.e) / math.sqrt(HD)
    for g in range(HEADS // 2):
        cols = slice(g * 2 * HD, (g + 1) * 2 * HD)
        vcols = slice(HEADS * HD + g * 2 * HD, HEADS * HD + (g + 1) * 2 * HD)
        q = mq_ref[:, cols] * scale
        k = mkv_ref[:, cols]
        v = mkv_ref[:, vcols]
        q3 = jnp.concatenate([q, q, q, hpad], axis=0)
        k2 = jnp.concatenate([k * even, k * odd], axis=0)
        v2 = jnp.concatenate([v * even, v * odd], axis=0)
        aq[(g + 1) * 2 * TAPS : (g + 2) * 2 * TAPS, :] = split_lanes(
            nt_dot_parts(k2, q3)
        )
        b = nt_dot_parts(nt_ref[:, cols], v2)
        bh = high(b)
        bb[g] = jnp.concatenate([bh, b - bh], axis=0).astype(jnp.bfloat16)


def shifted(x, by):
    lane = lax.broadcasted_iota(jnp.int32, x.shape, x.ndim - 1)
    width = x.shape[-1]
    if by == 1:
        return jnp.where(lane == 0, 0.0, pltpu.roll(x, 1, x.ndim - 1))
    return jnp.where(lane == width - 1, 0.0, pltpu.roll(x, width - 1, x.ndim - 1))


def is_even(axis):
    return lax.rem(lax.axis_index(axis), 2) == 0


def pack_kernel(own, first, second, after, rows, tail, lead):
    local = own.shape[0]
    even = is_even("space")
    kind = own.dtype
    for v in range(local):
        one = first[v].astype(jnp.float32)
        two = second[v].astype(jnp.float32)
        rows[v, 0] = jnp.where(even, two, one).astype(kind)
        rows[v, 1] = own[v]
        rows[v, 2] = jnp.where(even, one, two).astype(kind)
    for n in range(REACH):
        for i in range(3):
            tail[n, i] = rows[local - REACH + n, i]
            lead[n, i] = rows[n, i]


def patch_stack(rows):
    parts = []
    for row in rows:
        row = row.astype(jnp.float32)
        parts += [shifted(row, 1), row, shifted(row, -1)]
    patch = jnp.concatenate(parts, axis=0)
    pad = jnp.zeros((DEEP - 3 * TAPS, patch.shape[1]), jnp.float32)
    return jnp.concatenate([patch, patch, patch, pad], axis=0).astype(jnp.bfloat16)


def token_rate(gram_patches, patches):
    square = jnp.sum(gram_patches * patches, axis=0, keepdims=True) * (1.0 / 1024)
    return lax.rsqrt(jnp.maximum(square, 0.0) + 1e-6)


def store_keys(keyed, slots, kl, vl):
    w = keyed.shape[1] // len(slots)
    kh = high(keyed)
    low = keyed - kh
    sub = lax.broadcasted_iota(jnp.int32, (8, w), 0)
    for n, u in enumerate(slots):
        cols = slice(n * w, (n + 1) * w)
        onehot = (sub == u).astype(jnp.float32)
        h = kh[:, cols]
        r = low[:, cols]
        vl[:, cols] = jnp.concatenate([h, jnp.ones((8, w), jnp.float32), r], axis=0).astype(
            jnp.bfloat16
        )
        tall = jnp.concatenate(
            [h, onehot, r, h, jnp.zeros((DEEP - 3 * TAPS - 8, w), jnp.float32)], axis=0
        )
        kl[cols, :] = tall.T.astype(jnp.bfloat16)


def own_kernel(
    rows, gc, mq, mkv, nt, bias, qr, skip, bb, top, acc, p3, aq, kl, vl, sc, ex
):
    local, _, _, w = rows.shape
    aq[0 : 2 * TAPS, :] = gc[...]
    head_products(mq, mkv, nt, aq, bb)
    for v in range(local):
        p3[:, v * w : (v + 1) * w] = patch_stack([rows[v, i] for i in range(3)])
    asked = jnp.dot(aq[...], p3[...], preferred_element_type=jnp.float32)
    patches = p3[0:TAPS, :].astype(jnp.float32)
    rate = token_rate(asked[0:TAPS], patches)
    skip[...] = asked[TAPS : 2 * TAPS]
    store_keys(patches * rate, range(REACH, REACH + local), kl, vl)
    for v in range(local):
        for head in range(HEADS):
            q = asked[(head + 2) * TAPS : (head + 3) * TAPS, v * w : (v + 1) * w]
            q = q * rate[:, v * w : (v + 1) * w]
            h = high(q)
            qr[v, :, head * w : (head + 1) * w] = jnp.concatenate(
                [h, bias[v], h, q - h, jnp.zeros((DEEP - 3 * TAPS - 8, w), jnp.float32)], axis=0
            ).astype(jnp.bfloat16)
    spans = [(max(v - REACH, 0) * w, min(v + REACH + 1, local) * w) for v in range(local)]

    def scored(v):
        lo, hi = spans[v]
        sc[v % 2, 0 : hi - lo, :] = jnp.dot(
            kl[lo:hi, :], qr[v], preferred_element_type=jnp.float32
        )

    scored(0)
    for v in range(local):
        if v + 1 < local:
            scored(v + 1)
        lo, hi = spans[v]
        for head in range(HEADS):
            cols = slice(head * w, (head + 1) * w)
            scores = sc[v % 2, 0 : hi - lo, cols]
            largest = jnp.max(scores, axis=0, keepdims=True)
            top[v : v + 1, cols] = largest
            ex[v % 2, 0 : hi - lo, cols] = jnp.exp2(scores - largest).astype(jnp.bfloat16)
        gathered = jnp.dot(
            vl[:, lo:hi], ex[v % 2, 0 : hi - lo, :], preferred_element_type=jnp.float32
        )
        acc[v, 0:TAPS, :] = gathered[0:TAPS] + gathered[TAPS + 8 :]
        acc[v, TAPS:, :] = gathered[TAPS : TAPS + 8]


def mix_kernel(
    prev, nxt, gc, bb, qr, skip, top, acc,
    mine, late, early, p3, kl, vl, uh, ul, sc, ex,
):
    local, _, w = mine.shape
    for u in range(REACH):
        p3[:, u * w : (u + 1) * w] = patch_stack([prev[u, i] for i in range(3)])
        p3[:, (REACH + u) * w : (REACH + u + 1) * w] = patch_stack([nxt[u, i] for i in range(3)])
    gram = jnp.dot(gc[0:TAPS, :], p3[...], preferred_element_type=jnp.float32)
    patches = p3[0:TAPS, :].astype(jnp.float32)
    rate = token_rate(gram, patches)
    slots = [*range(REACH), *range(REACH + local, 2 * REACH + local)]
    store_keys(patches * rate, slots, kl, vl)
    spans = []
    for v in range(local):
        near = [n for n, u in enumerate(slots) if v <= u <= v + 2 * REACH]
        spans.append((near[0] * w, (near[-1] + 1) * w))
    for v, (lo, hi) in enumerate(spans):
        sc[v, 0 : hi - lo, :] = jnp.dot(
            kl[lo:hi, :], qr[v], preferred_element_type=jnp.float32
        )
    for v, (lo, hi) in enumerate(spans):
        fades = []
        for head in range(HEADS):
            cols = slice(head * w, (head + 1) * w)
            scores = sc[v, 0 : hi - lo, cols]
            before = top[v : v + 1, cols]
            largest = jnp.maximum(jnp.max(scores, axis=0, keepdims=True), before)
            fades.append(jnp.exp2(before - largest))
            ex[v, 0 : hi - lo, cols] = jnp.exp2(scores - largest).astype(jnp.bfloat16)
        fade = jnp.concatenate(fades, axis=1)
        gathered = jnp.dot(
            vl[:, lo:hi], ex[v, 0 : hi - lo, :], preferred_element_type=jnp.float32
        )
        weight = gathered[TAPS : TAPS + 1] + acc[v, TAPS : TAPS + 1, :] * fade
        mixed = gathered[0:TAPS] + gathered[TAPS + 8 :] + acc[v, 0:TAPS, :] * fade
        mixed = mixed * (1.0 / weight)
        for g in range(HEADS // 2):
            pair = mixed[:, g * 2 * w : (g + 1) * 2 * w]
            pair = jnp.concatenate([pair[:, :w], pair[:, w:]], axis=0)
            h = pair.astype(jnp.bfloat16)
            uh[g, :, v * w : (v + 1) * w] = h
            ul[g, :, v * w : (v + 1) * w] = (pair - h.astype(jnp.float32)).astype(jnp.bfloat16)
    z = skip[...]
    for g in range(HEADS // 2):
        y = jnp.dot(bb[g], uh[g], preferred_element_type=jnp.float32)
        z = z + y[:TAPS] + y[TAPS:]
        z = z + jnp.dot(bb[g, 0:TAPS, :], ul[g], preferred_element_type=jnp.float32)
    even = is_even("space")
    for v in range(local):
        parts = []
        for i in range(3):
            rows = z[i * 24 : (i + 1) * 24, v * w : (v + 1) * w]
            parts.append(shifted(rows[0:8], 1) + rows[8:16] + shifted(rows[16:24], -1))
        below, mine[v], above = parts
        early[v] = jnp.where(even, below, above)
        late[v] = jnp.where(even, above, below)


def pairs(count, start):
    both = []
    for i in range(start, count - 1, 2):
        both += [(i, i + 1), (i + 1, i)]
    return both


def on_device(
    latent,
    camera_edges,
    conv_in_weight,
    query_weight,
    key_value_weight,
    out_weight,
    conv_out_weight,
):
    local, channels, _, w = latent.shape
    span = local + 2 * REACH
    views = lax.axis_size("view")
    space = lax.axis_size("space")
    x = latent.reshape(local, channels, w)
    row_first = lax.ppermute(x, "space", pairs(space, 0))
    row_second = lax.ppermute(x, "space", pairs(space, 1))

    f32, bf16 = jnp.float32, jnp.bfloat16
    whole = pl.BlockSpec(memory_space=pltpu.VMEM)
    far = pl.BlockSpec(memory_space=pltpu.HBM)
    loaded = (
        camera_edges.T,
        conv_in_weight,
        conv_out_weight,
        query_weight,
        key_value_weight,
        out_weight,
    )
    gc, mq, mkv, nt, bias = pl.pallas_call(
        functools.partial(prepare_kernel, views),
        in_specs=[far] * len(loaded),
        out_specs=[whole] * 5,
        out_shape=[
            pltpu.VMEM((2 * TAPS, DEEP), bf16),
            pltpu.VMEM((TAPS, HEADS * HD), f32),
            pltpu.VMEM((TAPS, 2 * HEADS * HD), f32),
            pltpu.VMEM((TAPS, HEADS * HD), f32),
            pltpu.VMEM((local, span, w), f32),
        ],
        scratch_shapes=[
            pltpu.VMEM(a.shape, a.dtype)
            for a in (*loaded[:4], query_weight, query_weight, out_weight)
        ]
        + [pltpu.SemaphoreType.DMA((7,))],
        compiler_params=pltpu.CompilerParams(vmem_limit_bytes=60 * MIB),
        cost_estimate=pl.CostEstimate(
            flops=3_000_000_000, bytes_accessed=5_000_000, transcendentals=0
        ),
    )(*loaded)

    part = jax.ShapeDtypeStruct((REACH, 3, channels, w), bf16)
    rows, tail, lead = pl.pallas_call(
        pack_kernel,
        in_specs=[whole] * 3 + [pl.BlockSpec(memory_space=pl.ANY)],
        out_specs=[whole] * 3,
        out_shape=[jax.ShapeDtypeStruct((local, 3, channels, w), bf16), part, part],
        compiler_params=pltpu.CompilerParams(vmem_limit_bytes=4 * MIB),
    )(x, row_first, row_second, bias)
    prev = lax.ppermute(tail, "view", [(i, (i + 1) % views) for i in range(views)])
    nxt = lax.ppermute(lead, "view", [((i + 1) % views, i) for i in range(views)])

    keys_scratch = [
        pltpu.VMEM((local * w, DEEP), bf16),
        pltpu.VMEM((2 * TAPS + 8, local * w), bf16),
    ]
    qr, skip, bb, top, acc = pl.pallas_call(
        own_kernel,
        in_specs=[whole] * 6,
        out_specs=[whole] * 5,
        out_shape=[
            jax.ShapeDtypeStruct((local, DEEP, HEADS * w), bf16),
            jax.ShapeDtypeStruct((TAPS, local * w), f32),
            jax.ShapeDtypeStruct((HEADS // 2, 2 * TAPS, 2 * TAPS), bf16),
            jax.ShapeDtypeStruct((local, HEADS * w), f32),
            jax.ShapeDtypeStruct((local, TAPS + 8, HEADS * w), f32),
        ],
        scratch_shapes=[
            pltpu.VMEM((DEEP, local * w), bf16),
            pltpu.VMEM(((HEADS + 2) * TAPS, DEEP), bf16),
            *keys_scratch,
            pltpu.VMEM((2, local * w, HEADS * w), f32),
            pltpu.VMEM((2, local * w, HEADS * w), bf16),
        ],
        compiler_params=pltpu.CompilerParams(vmem_limit_bytes=24 * MIB),
        cost_estimate=pl.CostEstimate(
            flops=4_000_000_000, bytes_accessed=1_000_000, transcendentals=2_000_000
        ),
    )(rows, gc, mq, mkv, nt, bias)

    plane = jax.ShapeDtypeStruct((local, channels, w), f32)
    mine, late, early = pl.pallas_call(
        mix_kernel,
        in_specs=[whole] * 8,
        out_specs=[whole] * 3,
        out_shape=[plane] * 3,
        scratch_shapes=[
            pltpu.VMEM((DEEP, 2 * REACH * w), bf16),
            *keys_scratch,
            pltpu.VMEM((HEADS // 2, 2 * TAPS, local * w), bf16),
            pltpu.VMEM((HEADS // 2, 2 * TAPS, local * w), bf16),
            pltpu.VMEM((local, REACH * w, HEADS * w), f32),
            pltpu.VMEM((local, REACH * w, HEADS * w), bf16),
        ],
        compiler_params=pltpu.CompilerParams(vmem_limit_bytes=24 * MIB),
        cost_estimate=pl.CostEstimate(
            flops=3_000_000_000, bytes_accessed=1_000_000, transcendentals=1_000_000
        ),
    )(prev, nxt, gc, bb, qr, skip, top, acc)

    row_second = lax.ppermute(late, "space", pairs(space, 1))
    row_first = lax.ppermute(early, "space", pairs(space, 0))
    return (row_second + mine + row_first).reshape(local, channels, 1, w)


def solution(mesh):
    placed = (P("view", None, "space", None), P(), P(), P(), P(), P(), P())
    return jax.shard_map(
        on_device,
        mesh=mesh,
        in_specs=placed,
        out_specs=P("view", None, "space", None),
        check_vma=False,
    )
```

```python
import functools
import math

import jax
import jax.numpy as jnp
from jax import lax
from jax.experimental import pallas as pl
from jax.experimental.pallas import tpu as pltpu
from jax.sharding import PartitionSpec as P

HEADS = 8
HD = 64
REACH = 2
TAPS = 72
DEEP = 256
NEG_FILL = -1e30
MIB = 1024 * 1024


def nt_dot(a, b):
    return lax.dot_general(a, b, (((1,), (1,)), ((), ())), preferred_element_type=jnp.float32)


def high(x):
    return x.astype(jnp.bfloat16).astype(jnp.float32)


def split_lanes(x):
    lane = lax.broadcasted_iota(jnp.int32, x.shape, 1)
    first = high(x)
    rest = x - first
    second = high(rest)
    third = rest - second
    return jnp.where(lane < TAPS, first, jnp.where(lane < 2 * TAPS, second, third)).astype(
        jnp.bfloat16
    )


def flat_taps(ref):
    rows = [ref[i, j].astype(jnp.float32) for i in range(3) for j in range(3)]
    return jnp.concatenate(rows, axis=0)


def prepare_kernel(
    views, edges_hbm, conv_in_hbm, conv_out_hbm, wq_hbm, wkv_hbm,
    gc, mq, mkv, wt, bias, edges_ref, conv_in, conv_out, wq, wk, wv, sems,
):
    wide = HEADS * HD
    keys, values = slice(0, wide), slice(wide, 2 * wide)
    parts = (
        (edges_hbm, edges_ref),
        (conv_in_hbm, conv_in),
        (wq_hbm, wq),
        (wkv_hbm.at[:, keys], wk),
        (conv_out_hbm, conv_out),
        (wkv_hbm.at[:, values], wv),
    )
    copies = [pltpu.make_async_copy(src, dst, sems.at[n]) for n, (src, dst) in enumerate(parts)]
    for copy in copies:
        copy.start()
    local = bias.shape[0]
    span = bias.shape[1]
    total = views * local
    first = lax.axis_index("view") * local
    copies[0].wait()
    source = edges_ref[0:1, :]
    target = edges_ref[1:2, :]
    slot = lax.broadcasted_iota(jnp.int32, (span, 1), 0)
    near = first - REACH + slot
    near = jnp.where(near < 0, near + total, near)
    near = jnp.where(near >= total, near - total, near)
    for v in range(local):
        own = first + v
        hit = ((source == own) & (target == near)) | ((target == own) & (source == near))
        linked = jnp.max(hit.astype(jnp.float32), axis=1, keepdims=True)
        linked = jnp.where(slot == v + REACH, 1.0, linked)
        inside = (slot >= v) & (slot <= v + 2 * REACH)
        allowed = (linked > 0.5) & inside
        bias[v] = jnp.broadcast_to(jnp.where(allowed, 0.0, NEG_FILL), bias.shape[1:])
    copies[1].wait()
    wc = flat_taps(conv_in)
    wcb = wc.astype(jnp.bfloat16)
    copies[2].wait()
    mq[...] = jnp.dot(wcb, wq[...], preferred_element_type=jnp.float32)
    copies[3].wait()
    mkv[:, keys] = jnp.dot(wcb, wk[...], preferred_element_type=jnp.float32)
    copies[4].wait()
    taps = flat_taps(conv_out)
    wt[...] = taps.astype(jnp.bfloat16)
    pad = jnp.zeros((DEEP - 3 * TAPS, wc.shape[1]), jnp.float32)
    wc3 = jnp.concatenate([wc, wc, wc, pad], axis=0).astype(jnp.bfloat16)
    both = jnp.concatenate([wc, taps], axis=0).astype(jnp.bfloat16)
    gc[...] = split_lanes(nt_dot(both, wc3))
    copies[5].wait()
    mkv[:, values] = jnp.dot(wcb, wv[...], preferred_element_type=jnp.float32)


def nt_dot_parts(a, b):
    ah, bh = high(a), high(b)
    left = jnp.concatenate([ah, a - ah, ah], axis=1).astype(jnp.bfloat16)
    right = jnp.concatenate([bh, bh, b - bh], axis=1).astype(jnp.bfloat16)
    return nt_dot(left, right)


def head_products(mq_ref, mkv_ref, nt, aq, bb):
    lane = lax.broadcasted_iota(jnp.int32, (TAPS, 2 * HD), 1)
    even = (lane < HD).astype(jnp.float32)
    odd = 1.0 - even
    hpad = jnp.zeros((DEEP - 3 * TAPS, 2 * HD), jnp.float32)
    scale = math.log2(math.e) / math.sqrt(HD)
    for g in range(HEADS // 2):
        cols = slice(g * 2 * HD, (g + 1) * 2 * HD)
        vcols = slice(HEADS * HD + g * 2 * HD, HEADS * HD + (g + 1) * 2 * HD)
        q = mq_ref[:, cols] * scale
        k = mkv_ref[:, cols]
        v = mkv_ref[:, vcols]
        q3 = jnp.concatenate([q, q, q, hpad], axis=0)
        k2 = jnp.concatenate([k * even, k * odd], axis=0)
        v2 = jnp.concatenate([v * even, v * odd], axis=0)
        aq[(g + 1) * 2 * TAPS : (g + 2) * 2 * TAPS, :] = split_lanes(
            nt_dot_parts(k2, q3)
        )
        b = nt_dot_parts(nt[:, cols], v2)
        bh = high(b)
        bb[g] = jnp.concatenate([bh, b - bh], axis=0).astype(jnp.bfloat16)


def shifted(x, by):
    lane = lax.broadcasted_iota(jnp.int32, x.shape, x.ndim - 1)
    width = x.shape[-1]
    if by == 1:
        return jnp.where(lane == 0, 0.0, pltpu.roll(x, 1, x.ndim - 1))
    return jnp.where(lane == width - 1, 0.0, pltpu.roll(x, width - 1, x.ndim - 1))


def is_even(axis):
    return lax.rem(lax.axis_index(axis), 2) == 0


def pack_kernel(own, first, second, after, rows, tail, lead):
    local = own.shape[0]
    even = is_even("space")
    kind = own.dtype
    for v in range(local):
        one = first[v].astype(jnp.float32)
        two = second[v].astype(jnp.float32)
        rows[v, 0] = jnp.where(even, two, one).astype(kind)
        rows[v, 1] = own[v]
        rows[v, 2] = jnp.where(even, one, two).astype(kind)
    for n in range(REACH):
        for i in range(3):
            tail[n, i] = rows[local - REACH + n, i]
            lead[n, i] = rows[n, i]


def patch_stack(rows):
    parts = []
    for row in rows:
        row = row.astype(jnp.float32)
        parts += [shifted(row, 1), row, shifted(row, -1)]
    patch = jnp.concatenate(parts, axis=0)
    pad = jnp.zeros((DEEP - 3 * TAPS, patch.shape[1]), jnp.float32)
    return jnp.concatenate([patch, patch, patch, pad], axis=0).astype(jnp.bfloat16)


def token_rate(gram_patches, patches):
    square = jnp.sum(gram_patches * patches, axis=0, keepdims=True) * (1.0 / 1024)
    return lax.rsqrt(jnp.maximum(square, 0.0) + 1e-6)


def store_keys(keyed, slots, kl, vl):
    w = keyed.shape[1] // len(slots)
    kh = high(keyed)
    low = keyed - kh
    sub = lax.broadcasted_iota(jnp.int32, (8, w), 0)
    for n, u in enumerate(slots):
        cols = slice(n * w, (n + 1) * w)
        onehot = (sub == u).astype(jnp.float32)
        h = kh[:, cols]
        r = low[:, cols]
        vl[:, cols] = jnp.concatenate([h, jnp.ones((8, w), jnp.float32), r], axis=0).astype(
            jnp.bfloat16
        )
        tall = jnp.concatenate(
            [h, onehot, r, h, jnp.zeros((DEEP - 3 * TAPS - 8, w), jnp.float32)], axis=0
        )
        kl[cols, :] = tall.T.astype(jnp.bfloat16)


def own_kernel(
    rows, gc, mq, mkv, wt, wo, bias, qr, skip, bb, top, acc, p3, aq, kl, vl, sc, ex
):
    local, _, _, w = rows.shape
    aq[0 : 2 * TAPS, :] = gc[...]
    head_products(mq, mkv, nt_dot(wt[...], wo[...]), aq, bb)
    for v in range(local):
        p3[:, v * w : (v + 1) * w] = patch_stack([rows[v, i] for i in range(3)])
    asked = jnp.dot(aq[...], p3[...], preferred_element_type=jnp.float32)
    patches = p3[0:TAPS, :].astype(jnp.float32)
    rate = token_rate(asked[0:TAPS], patches)
    skip[...] = asked[TAPS : 2 * TAPS]
    store_keys(patches * rate, range(REACH, REACH + local), kl, vl)
    for v in range(local):
        for head in range(HEADS):
            q = asked[(head + 2) * TAPS : (head + 3) * TAPS, v * w : (v + 1) * w]
            q = q * rate[:, v * w : (v + 1) * w]
            h = high(q)
            qr[v, :, head * w : (head + 1) * w] = jnp.concatenate(
                [h, bias[v], h, q - h, jnp.zeros((DEEP - 3 * TAPS - 8, w), jnp.float32)], axis=0
            ).astype(jnp.bfloat16)
    spans = [(max(v - REACH, 0) * w, min(v + REACH + 1, local) * w) for v in range(local)]

    def scored(v):
        lo, hi = spans[v]
        sc[v % 2, 0 : hi - lo, :] = jnp.dot(
            kl[lo:hi, :], qr[v], preferred_element_type=jnp.float32
        )

    scored(0)
    for v in range(local):
        if v + 1 < local:
            scored(v + 1)
        lo, hi = spans[v]
        for head in range(HEADS):
            cols = slice(head * w, (head + 1) * w)
            scores = sc[v % 2, 0 : hi - lo, cols]
            largest = jnp.max(scores, axis=0, keepdims=True)
            top[v : v + 1, cols] = largest
            ex[v % 2, 0 : hi - lo, cols] = jnp.exp2(scores - largest).astype(jnp.bfloat16)
        gathered = jnp.dot(
            vl[:, lo:hi], ex[v % 2, 0 : hi - lo, :], preferred_element_type=jnp.float32
        )
        acc[v, 0:TAPS, :] = gathered[0:TAPS] + gathered[TAPS + 8 :]
        acc[v, TAPS:, :] = gathered[TAPS : TAPS + 8]


def mix_kernel(
    prev, nxt, gc, bb, qr, skip, top, acc,
    mine, late, early, p3, kl, vl, uh, ul, sc, ex,
):
    local, _, w = mine.shape
    for u in range(REACH):
        p3[:, u * w : (u + 1) * w] = patch_stack([prev[u, i] for i in range(3)])
        p3[:, (REACH + u) * w : (REACH + u + 1) * w] = patch_stack([nxt[u, i] for i in range(3)])
    gram = jnp.dot(gc[0:TAPS, :], p3[...], preferred_element_type=jnp.float32)
    patches = p3[0:TAPS, :].astype(jnp.float32)
    rate = token_rate(gram, patches)
    slots = [*range(REACH), *range(REACH + local, 2 * REACH + local)]
    store_keys(patches * rate, slots, kl, vl)
    spans = []
    for v in range(local):
        near = [n for n, u in enumerate(slots) if v <= u <= v + 2 * REACH]
        spans.append((near[0] * w, (near[-1] + 1) * w))
    for v, (lo, hi) in enumerate(spans):
        sc[v, 0 : hi - lo, :] = jnp.dot(
            kl[lo:hi, :], qr[v], preferred_element_type=jnp.float32
        )
    for v, (lo, hi) in enumerate(spans):
        fades = []
        for head in range(HEADS):
            cols = slice(head * w, (head + 1) * w)
            scores = sc[v, 0 : hi - lo, cols]
            before = top[v : v + 1, cols]
            largest = jnp.maximum(jnp.max(scores, axis=0, keepdims=True), before)
            fades.append(jnp.exp2(before - largest))
            ex[v, 0 : hi - lo, cols] = jnp.exp2(scores - largest).astype(jnp.bfloat16)
        fade = jnp.concatenate(fades, axis=1)
        gathered = jnp.dot(
            vl[:, lo:hi], ex[v, 0 : hi - lo, :], preferred_element_type=jnp.float32
        )
        weight = gathered[TAPS : TAPS + 1] + acc[v, TAPS : TAPS + 1, :] * fade
        mixed = gathered[0:TAPS] + gathered[TAPS + 8 :] + acc[v, 0:TAPS, :] * fade
        mixed = mixed * (1.0 / weight)
        for g in range(HEADS // 2):
            pair = mixed[:, g * 2 * w : (g + 1) * 2 * w]
            pair = jnp.concatenate([pair[:, :w], pair[:, w:]], axis=0)
            h = pair.astype(jnp.bfloat16)
            uh[g, :, v * w : (v + 1) * w] = h
            ul[g, :, v * w : (v + 1) * w] = (pair - h.astype(jnp.float32)).astype(jnp.bfloat16)
    z = skip[...]
    for g in range(HEADS // 2):
        y = jnp.dot(bb[g], uh[g], preferred_element_type=jnp.float32)
        z = z + y[:TAPS] + y[TAPS:]
        z = z + jnp.dot(bb[g, 0:TAPS, :], ul[g], preferred_element_type=jnp.float32)
    even = is_even("space")
    for v in range(local):
        parts = []
        for i in range(3):
            rows = z[i * 24 : (i + 1) * 24, v * w : (v + 1) * w]
            parts.append(shifted(rows[0:8], 1) + rows[8:16] + shifted(rows[16:24], -1))
        below, mine[v], above = parts
        early[v] = jnp.where(even, below, above)
        late[v] = jnp.where(even, above, below)


def pairs(count, start):
    both = []
    for i in range(start, count - 1, 2):
        both += [(i, i + 1), (i + 1, i)]
    return both


def on_device(
    latent,
    camera_edges,
    conv_in_weight,
    query_weight,
    key_value_weight,
    out_weight,
    conv_out_weight,
):
    local, channels, _, w = latent.shape
    span = local + 2 * REACH
    views = lax.axis_size("view")
    space = lax.axis_size("space")
    x = latent.reshape(local, channels, w)
    row_first = lax.ppermute(x, "space", pairs(space, 0))
    row_second = lax.ppermute(x, "space", pairs(space, 1))

    f32, bf16 = jnp.float32, jnp.bfloat16
    whole = pl.BlockSpec(memory_space=pltpu.VMEM)
    far = pl.BlockSpec(memory_space=pltpu.HBM)
    loaded = (
        camera_edges.T,
        conv_in_weight,
        conv_out_weight,
        query_weight,
        key_value_weight,
    )
    gc, mq, mkv, wt, bias = pl.pallas_call(
        functools.partial(prepare_kernel, views),
        in_specs=[far] * len(loaded),
        out_specs=[whole] * 5,
        out_shape=[
            pltpu.VMEM((2 * TAPS, DEEP), bf16),
            pltpu.VMEM((TAPS, HEADS * HD), f32),
            pltpu.VMEM((TAPS, 2 * HEADS * HD), f32),
            pltpu.VMEM((TAPS, out_weight.shape[1]), bf16),
            pltpu.VMEM((local, span, w), f32),
        ],
        scratch_shapes=[
            pltpu.VMEM(a.shape, a.dtype)
            for a in (*loaded[:4], query_weight, query_weight)
        ]
        + [pltpu.SemaphoreType.DMA((6,))],
        compiler_params=pltpu.CompilerParams(vmem_limit_bytes=60 * MIB),
        cost_estimate=pl.CostEstimate(
            flops=3_000_000_000, bytes_accessed=5_000_000, transcendentals=0
        ),
    )(*loaded)

    part = jax.ShapeDtypeStruct((REACH, 3, channels, w), bf16)
    rows, tail, lead = pl.pallas_call(
        pack_kernel,
        in_specs=[whole] * 3 + [pl.BlockSpec(memory_space=pl.ANY)],
        out_specs=[whole] * 3,
        out_shape=[jax.ShapeDtypeStruct((local, 3, channels, w), bf16), part, part],
        compiler_params=pltpu.CompilerParams(vmem_limit_bytes=4 * MIB),
    )(x, row_first, row_second, bias)
    prev = lax.ppermute(tail, "view", [(i, (i + 1) % views) for i in range(views)])
    nxt = lax.ppermute(lead, "view", [((i + 1) % views, i) for i in range(views)])

    keys_scratch = [
        pltpu.VMEM((local * w, DEEP), bf16),
        pltpu.VMEM((2 * TAPS + 8, local * w), bf16),
    ]
    qr, skip, bb, top, acc = pl.pallas_call(
        own_kernel,
        in_specs=[whole] * 7,
        out_specs=[whole] * 5,
        out_shape=[
            jax.ShapeDtypeStruct((local, DEEP, HEADS * w), bf16),
            jax.ShapeDtypeStruct((TAPS, local * w), f32),
            jax.ShapeDtypeStruct((HEADS // 2, 2 * TAPS, 2 * TAPS), bf16),
            jax.ShapeDtypeStruct((local, HEADS * w), f32),
            jax.ShapeDtypeStruct((local, TAPS + 8, HEADS * w), f32),
        ],
        scratch_shapes=[
            pltpu.VMEM((DEEP, local * w), bf16),
            pltpu.VMEM(((HEADS + 2) * TAPS, DEEP), bf16),
            *keys_scratch,
            pltpu.VMEM((2, local * w, HEADS * w), f32),
            pltpu.VMEM((2, local * w, HEADS * w), bf16),
        ],
        compiler_params=pltpu.CompilerParams(vmem_limit_bytes=24 * MIB),
        cost_estimate=pl.CostEstimate(
            flops=4_000_000_000, bytes_accessed=1_000_000, transcendentals=2_000_000
        ),
    )(rows, gc, mq, mkv, wt, out_weight, bias)

    plane = jax.ShapeDtypeStruct((local, channels, w), f32)
    mine, late, early = pl.pallas_call(
        mix_kernel,
        in_specs=[whole] * 8,
        out_specs=[whole] * 3,
        out_shape=[plane] * 3,
        scratch_shapes=[
            pltpu.VMEM((DEEP, 2 * REACH * w), bf16),
            *keys_scratch,
            pltpu.VMEM((HEADS // 2, 2 * TAPS, local * w), bf16),
            pltpu.VMEM((HEADS // 2, 2 * TAPS, local * w), bf16),
            pltpu.VMEM((local, REACH * w, HEADS * w), f32),
            pltpu.VMEM((local, REACH * w, HEADS * w), bf16),
        ],
        compiler_params=pltpu.CompilerParams(vmem_limit_bytes=24 * MIB),
        cost_estimate=pl.CostEstimate(
            flops=3_000_000_000, bytes_accessed=1_000_000, transcendentals=1_000_000
        ),
    )(prev, nxt, gc, bb, qr, skip, top, acc)

    row_second = lax.ppermute(late, "space", pairs(space, 1))
    row_first = lax.ppermute(early, "space", pairs(space, 0))
    return (row_second + mine + row_first).reshape(local, channels, 1, w)


def solution(mesh):
    placed = (P("view", None, "space", None), P(), P(), P(), P(), P(), P())
    return jax.shard_map(
        on_device,
        mesh=mesh,
        in_specs=placed,
        out_specs=P("view", None, "space", None),
        check_vma=False,
    )
```

```python
import functools
import math

import jax
import jax.numpy as jnp
from jax import lax
from jax.experimental import pallas as pl
from jax.experimental.pallas import tpu as pltpu
from jax.sharding import PartitionSpec as P

HEADS = 8
HD = 64
REACH = 2
TAPS = 72
DEEP = 256
NEG_FILL = -1e30
MIB = 1024 * 1024


def nt_dot(a, b):
    return lax.dot_general(a, b, (((1,), (1,)), ((), ())), preferred_element_type=jnp.float32)


def high(x):
    return x.astype(jnp.bfloat16).astype(jnp.float32)


def split_lanes(x):
    lane = lax.broadcasted_iota(jnp.int32, x.shape, 1)
    first = high(x)
    rest = x - first
    second = high(rest)
    third = rest - second
    return jnp.where(lane < TAPS, first, jnp.where(lane < 2 * TAPS, second, third)).astype(
        jnp.bfloat16
    )


def flat_taps(ref):
    rows = [ref[i, j].astype(jnp.float32) for i in range(3) for j in range(3)]
    return jnp.concatenate(rows, axis=0)


def prepare_kernel(
    views, edges_hbm, conv_in_hbm, conv_out_hbm, wq_hbm, wkv_hbm,
    gc, mq, mk, taps, bias, edges_ref, conv_in, conv_out, wq, wk, sems,
):
    parts = (
        (edges_hbm, edges_ref),
        (conv_in_hbm, conv_in),
        (wq_hbm, wq),
        (wkv_hbm.at[:, : HEADS * HD], wk),
        (conv_out_hbm, conv_out),
    )
    copies = [pltpu.make_async_copy(src, dst, sems.at[n]) for n, (src, dst) in enumerate(parts)]
    for copy in copies:
        copy.start()
    local = bias.shape[0]
    span = bias.shape[1]
    total = views * local
    first = lax.axis_index("view") * local
    copies[0].wait()
    source = edges_ref[0:1, :]
    target = edges_ref[1:2, :]
    slot = lax.broadcasted_iota(jnp.int32, (span, 1), 0)
    near = first - REACH + slot
    near = jnp.where(near < 0, near + total, near)
    near = jnp.where(near >= total, near - total, near)
    for v in range(local):
        own = first + v
        hit = ((source == own) & (target == near)) | ((target == own) & (source == near))
        linked = jnp.max(hit.astype(jnp.float32), axis=1, keepdims=True)
        linked = jnp.where(slot == v + REACH, 1.0, linked)
        inside = (slot >= v) & (slot <= v + 2 * REACH)
        allowed = (linked > 0.5) & inside
        bias[v] = jnp.broadcast_to(jnp.where(allowed, 0.0, NEG_FILL), bias.shape[1:])
    copies[1].wait()
    wc = flat_taps(conv_in)
    wcb = wc.astype(jnp.bfloat16)
    copies[2].wait()
    mq[...] = jnp.dot(wcb, wq[...], preferred_element_type=jnp.float32)
    copies[3].wait()
    mk[...] = jnp.dot(wcb, wk[...], preferred_element_type=jnp.float32)
    copies[4].wait()
    wt = flat_taps(conv_out)
    pad = jnp.zeros((DEEP - 3 * TAPS, wc.shape[1]), jnp.float32)
    wc3 = jnp.concatenate([wc, wc, wc, pad], axis=0).astype(jnp.bfloat16)
    taps[...] = jnp.concatenate([wc, wt], axis=0).astype(jnp.bfloat16)
    gc[...] = split_lanes(nt_dot(taps[...], wc3))


def nt_dot_parts(a, b):
    ah, bh = high(a), high(b)
    left = jnp.concatenate([ah, a - ah, ah], axis=1).astype(jnp.bfloat16)
    right = jnp.concatenate([bh, bh, b - bh], axis=1).astype(jnp.bfloat16)
    return nt_dot(left, right)


def head_pair(g):
    lane = lax.broadcasted_iota(jnp.int32, (TAPS, 2 * HD), 1)
    even = (lane < HD).astype(jnp.float32)
    return slice(g * 2 * HD, (g + 1) * 2 * HD), even, 1.0 - even


def score_products(mq, mk, aq):
    pad = jnp.zeros((DEEP - 3 * TAPS, 2 * HD), jnp.float32)
    scale = math.log2(math.e) / math.sqrt(HD)
    for g in range(HEADS // 2):
        cols, even, odd = head_pair(g)
        q = mq[:, cols] * scale
        k = mk[:, cols]
        q3 = jnp.concatenate([q, q, q, pad], axis=0)
        k2 = jnp.concatenate([k * even, k * odd], axis=0)
        aq[(g + 1) * 2 * TAPS : (g + 2) * 2 * TAPS, :] = split_lanes(nt_dot_parts(k2, q3))


def value_products(mv, nt, bb):
    for g in range(HEADS // 2):
        cols, even, odd = head_pair(g)
        v = mv[:, cols]
        v2 = jnp.concatenate([v * even, v * odd], axis=0)
        b = nt_dot_parts(nt[:, cols], v2)
        bh = high(b)
        bb[g] = jnp.concatenate([bh, b - bh], axis=0).astype(jnp.bfloat16)


def shifted(x, by):
    lane = lax.broadcasted_iota(jnp.int32, x.shape, x.ndim - 1)
    width = x.shape[-1]
    if by == 1:
        return jnp.where(lane == 0, 0.0, pltpu.roll(x, 1, x.ndim - 1))
    return jnp.where(lane == width - 1, 0.0, pltpu.roll(x, width - 1, x.ndim - 1))


def is_even(axis):
    return lax.rem(lax.axis_index(axis), 2) == 0


def pack_kernel(own, first, second, after, rows, tail, lead):
    local = own.shape[0]
    even = is_even("space")
    kind = own.dtype
    for v in range(local):
        one = first[v].astype(jnp.float32)
        two = second[v].astype(jnp.float32)
        rows[v, 0] = jnp.where(even, two, one).astype(kind)
        rows[v, 1] = own[v]
        rows[v, 2] = jnp.where(even, one, two).astype(kind)
    for n in range(REACH):
        for i in range(3):
            tail[n, i] = rows[local - REACH + n, i]
            lead[n, i] = rows[n, i]


def patch_stack(rows):
    parts = []
    for row in rows:
        row = row.astype(jnp.float32)
        parts += [shifted(row, 1), row, shifted(row, -1)]
    patch = jnp.concatenate(parts, axis=0)
    pad = jnp.zeros((DEEP - 3 * TAPS, patch.shape[1]), jnp.float32)
    return jnp.concatenate([patch, patch, patch, pad], axis=0).astype(jnp.bfloat16)


def token_rate(gram_patches, patches):
    square = jnp.sum(gram_patches * patches, axis=0, keepdims=True) * (1.0 / 1024)
    return lax.rsqrt(jnp.maximum(square, 0.0) + 1e-6)


def store_keys(keyed, slots, kl, vl):
    w = keyed.shape[1] // len(slots)
    kh = high(keyed)
    low = keyed - kh
    sub = lax.broadcasted_iota(jnp.int32, (8, w), 0)
    for n, u in enumerate(slots):
        cols = slice(n * w, (n + 1) * w)
        onehot = (sub == u).astype(jnp.float32)
        h = kh[:, cols]
        r = low[:, cols]
        vl[:, cols] = jnp.concatenate([h, jnp.ones((8, w), jnp.float32), r], axis=0).astype(
            jnp.bfloat16
        )
        tall = jnp.concatenate(
            [h, onehot, r, h, jnp.zeros((DEEP - 3 * TAPS - 8, w), jnp.float32)], axis=0
        )
        kl[cols, :] = tall.T.astype(jnp.bfloat16)


def own_kernel(
    rows, gc, mq, mk, taps, bias, wkv_hbm, wo_hbm,
    qr, skip, bb, top, acc, p3, aq, kl, vl, sc, ex, wv, wo, sems,
):
    local, _, _, w = rows.shape
    copies = [
        pltpu.make_async_copy(wkv_hbm.at[:, HEADS * HD :], wv, sems.at[0]),
        pltpu.make_async_copy(wo_hbm, wo, sems.at[1]),
    ]
    for copy in copies:
        copy.start()
    aq[0 : 2 * TAPS, :] = gc[...]
    score_products(mq, mk, aq)
    for v in range(local):
        p3[:, v * w : (v + 1) * w] = patch_stack([rows[v, i] for i in range(3)])
    asked = jnp.dot(aq[...], p3[...], preferred_element_type=jnp.float32)
    patches = p3[0:TAPS, :].astype(jnp.float32)
    rate = token_rate(asked[0:TAPS], patches)
    skip[...] = asked[TAPS : 2 * TAPS]
    store_keys(patches * rate, range(REACH, REACH + local), kl, vl)
    for v in range(local):
        for head in range(HEADS):
            q = asked[(head + 2) * TAPS : (head + 3) * TAPS, v * w : (v + 1) * w]
            q = q * rate[:, v * w : (v + 1) * w]
            h = high(q)
            qr[v, :, head * w : (head + 1) * w] = jnp.concatenate(
                [h, bias[v], h, q - h, jnp.zeros((DEEP - 3 * TAPS - 8, w), jnp.float32)], axis=0
            ).astype(jnp.bfloat16)
    spans = [(max(v - REACH, 0) * w, min(v + REACH + 1, local) * w) for v in range(local)]

    def scored(v):
        lo, hi = spans[v]
        sc[v % 2, 0 : hi - lo, :] = jnp.dot(
            kl[lo:hi, :], qr[v], preferred_element_type=jnp.float32
        )

    scored(0)
    for v in range(local):
        if v + 1 < local:
            scored(v + 1)
        lo, hi = spans[v]
        for head in range(HEADS):
            cols = slice(head * w, (head + 1) * w)
            scores = sc[v % 2, 0 : hi - lo, cols]
            largest = jnp.max(scores, axis=0, keepdims=True)
            top[v : v + 1, cols] = largest
            ex[v % 2, 0 : hi - lo, cols] = jnp.exp2(scores - largest).astype(jnp.bfloat16)
        gathered = jnp.dot(
            vl[:, lo:hi], ex[v % 2, 0 : hi - lo, :], preferred_element_type=jnp.float32
        )
        acc[v, 0:TAPS, :] = gathered[0:TAPS] + gathered[TAPS + 8 :]
        acc[v, TAPS:, :] = gathered[TAPS : TAPS + 8]
    copies[0].wait()
    mv = jnp.dot(taps[0:TAPS, :], wv[...], preferred_element_type=jnp.float32)
    copies[1].wait()
    value_products(mv, nt_dot(taps[TAPS:, :], wo[...]), bb)


def mix_kernel(
    prev, nxt, gc, bb, qr, skip, top, acc,
    mine, late, early, p3, kl, vl, uh, ul, sc, ex,
):
    local, _, w = mine.shape
    for u in range(REACH):
        p3[:, u * w : (u + 1) * w] = patch_stack([prev[u, i] for i in range(3)])
        p3[:, (REACH + u) * w : (REACH + u + 1) * w] = patch_stack([nxt[u, i] for i in range(3)])
    gram = jnp.dot(gc[0:TAPS, :], p3[...], preferred_element_type=jnp.float32)
    patches = p3[0:TAPS, :].astype(jnp.float32)
    rate = token_rate(gram, patches)
    slots = [*range(REACH), *range(REACH + local, 2 * REACH + local)]
    store_keys(patches * rate, slots, kl, vl)
    spans = []
    for v in range(local):
        near = [n for n, u in enumerate(slots) if v <= u <= v + 2 * REACH]
        spans.append((near[0] * w, (near[-1] + 1) * w))
    for v, (lo, hi) in enumerate(spans):
        sc[v, 0 : hi - lo, :] = jnp.dot(
            kl[lo:hi, :], qr[v], preferred_element_type=jnp.float32
        )
    for v, (lo, hi) in enumerate(spans):
        fades = []
        for head in range(HEADS):
            cols = slice(head * w, (head + 1) * w)
            scores = sc[v, 0 : hi - lo, cols]
            before = top[v : v + 1, cols]
            largest = jnp.maximum(jnp.max(scores, axis=0, keepdims=True), before)
            fades.append(jnp.exp2(before - largest))
            ex[v, 0 : hi - lo, cols] = jnp.exp2(scores - largest).astype(jnp.bfloat16)
        fade = jnp.concatenate(fades, axis=1)
        gathered = jnp.dot(
            vl[:, lo:hi], ex[v, 0 : hi - lo, :], preferred_element_type=jnp.float32
        )
        weight = gathered[TAPS : TAPS + 1] + acc[v, TAPS : TAPS + 1, :] * fade
        mixed = gathered[0:TAPS] + gathered[TAPS + 8 :] + acc[v, 0:TAPS, :] * fade
        mixed = mixed * (1.0 / weight)
        for g in range(HEADS // 2):
            pair = mixed[:, g * 2 * w : (g + 1) * 2 * w]
            pair = jnp.concatenate([pair[:, :w], pair[:, w:]], axis=0)
            h = pair.astype(jnp.bfloat16)
            uh[g, :, v * w : (v + 1) * w] = h
            ul[g, :, v * w : (v + 1) * w] = (pair - h.astype(jnp.float32)).astype(jnp.bfloat16)
    z = skip[...]
    for g in range(HEADS // 2):
        y = jnp.dot(bb[g], uh[g], preferred_element_type=jnp.float32)
        z = z + y[:TAPS] + y[TAPS:]
        z = z + jnp.dot(bb[g, 0:TAPS, :], ul[g], preferred_element_type=jnp.float32)
    even = is_even("space")
    for v in range(local):
        parts = []
        for i in range(3):
            rows = z[i * 24 : (i + 1) * 24, v * w : (v + 1) * w]
            parts.append(shifted(rows[0:8], 1) + rows[8:16] + shifted(rows[16:24], -1))
        below, mine[v], above = parts
        early[v] = jnp.where(even, below, above)
        late[v] = jnp.where(even, above, below)


def pairs(count, start):
    both = []
    for i in range(start, count - 1, 2):
        both += [(i, i + 1), (i + 1, i)]
    return both


def on_device(
    latent,
    camera_edges,
    conv_in_weight,
    query_weight,
    key_value_weight,
    out_weight,
    conv_out_weight,
):
    local, channels, _, w = latent.shape
    span = local + 2 * REACH
    views = lax.axis_size("view")
    space = lax.axis_size("space")
    x = latent.reshape(local, channels, w)
    row_first = lax.ppermute(x, "space", pairs(space, 0))
    row_second = lax.ppermute(x, "space", pairs(space, 1))

    f32, bf16 = jnp.float32, jnp.bfloat16
    whole = pl.BlockSpec(memory_space=pltpu.VMEM)
    far = pl.BlockSpec(memory_space=pltpu.HBM)
    loaded = (
        camera_edges.T,
        conv_in_weight,
        conv_out_weight,
        query_weight,
        key_value_weight,
    )
    gc, mq, mk, taps, bias = pl.pallas_call(
        functools.partial(prepare_kernel, views),
        in_specs=[far] * len(loaded),
        out_specs=[whole] * 5,
        out_shape=[
            pltpu.VMEM((2 * TAPS, DEEP), bf16),
            pltpu.VMEM((TAPS, HEADS * HD), f32),
            pltpu.VMEM((TAPS, HEADS * HD), f32),
            pltpu.VMEM((2 * TAPS, out_weight.shape[1]), bf16),
            pltpu.VMEM((local, span, w), f32),
        ],
        scratch_shapes=[
            pltpu.VMEM(a.shape, a.dtype)
            for a in (*loaded[:4], query_weight)
        ]
        + [pltpu.SemaphoreType.DMA((5,))],
        compiler_params=pltpu.CompilerParams(vmem_limit_bytes=60 * MIB),
        cost_estimate=pl.CostEstimate(
            flops=3_000_000_000, bytes_accessed=5_000_000, transcendentals=0
        ),
    )(*loaded)

    part = jax.ShapeDtypeStruct((REACH, 3, channels, w), bf16)
    rows, tail, lead = pl.pallas_call(
        pack_kernel,
        in_specs=[whole] * 3 + [pl.BlockSpec(memory_space=pl.ANY)],
        out_specs=[whole] * 3,
        out_shape=[pltpu.VMEM((local, 3, channels, w), bf16), part, part],
        compiler_params=pltpu.CompilerParams(vmem_limit_bytes=4 * MIB),
    )(x, row_first, row_second, bias)
    prev = lax.ppermute(tail, "view", [(i, (i + 1) % views) for i in range(views)])
    nxt = lax.ppermute(lead, "view", [((i + 1) % views, i) for i in range(views)])

    keys_scratch = [
        pltpu.VMEM((local * w, DEEP), bf16),
        pltpu.VMEM((2 * TAPS + 8, local * w), bf16),
    ]
    qr, skip, bb, top, acc = pl.pallas_call(
        own_kernel,
        in_specs=[whole] * 6 + [far] * 2,
        out_specs=[whole] * 5,
        out_shape=[
            pltpu.VMEM((local, DEEP, HEADS * w), bf16),
            pltpu.VMEM((TAPS, local * w), f32),
            pltpu.VMEM((HEADS // 2, 2 * TAPS, 2 * TAPS), bf16),
            pltpu.VMEM((local, HEADS * w), f32),
            pltpu.VMEM((local, TAPS + 8, HEADS * w), f32),
        ],
        scratch_shapes=[
            pltpu.VMEM((DEEP, local * w), bf16),
            pltpu.VMEM(((HEADS + 2) * TAPS, DEEP), bf16),
            *keys_scratch,
            pltpu.VMEM((2, local * w, HEADS * w), f32),
            pltpu.VMEM((2, local * w, HEADS * w), bf16),
            pltpu.VMEM(query_weight.shape, bf16),
            pltpu.VMEM(out_weight.shape, bf16),
            pltpu.SemaphoreType.DMA((2,)),
        ],
        compiler_params=pltpu.CompilerParams(vmem_limit_bytes=49 * MIB),
        cost_estimate=pl.CostEstimate(
            flops=4_000_000_000, bytes_accessed=1_000_000, transcendentals=2_000_000
        ),
    )(rows, gc, mq, mk, taps, bias, key_value_weight, out_weight)

    plane = jax.ShapeDtypeStruct((local, channels, w), f32)
    mine, late, early = pl.pallas_call(
        mix_kernel,
        in_specs=[whole] * 8,
        out_specs=[whole] * 3,
        out_shape=[plane] * 3,
        scratch_shapes=[
            pltpu.VMEM((DEEP, 2 * REACH * w), bf16),
            *keys_scratch,
            pltpu.VMEM((HEADS // 2, 2 * TAPS, local * w), bf16),
            pltpu.VMEM((HEADS // 2, 2 * TAPS, local * w), bf16),
            pltpu.VMEM((local, REACH * w, HEADS * w), f32),
            pltpu.VMEM((local, REACH * w, HEADS * w), bf16),
        ],
        compiler_params=pltpu.CompilerParams(vmem_limit_bytes=24 * MIB),
        cost_estimate=pl.CostEstimate(
            flops=3_000_000_000, bytes_accessed=1_000_000, transcendentals=1_000_000
        ),
    )(prev, nxt, gc, bb, qr, skip, top, acc)

    row_second = lax.ppermute(late, "space", pairs(space, 1))
    row_first = lax.ppermute(early, "space", pairs(space, 0))
    return (row_second + mine + row_first).reshape(local, channels, 1, w)


def solution(mesh):
    placed = (P("view", None, "space", None), P(), P(), P(), P(), P(), P())
    return jax.shard_map(
        on_device,
        mesh=mesh,
        in_specs=placed,
        out_specs=P("view", None, "space", None),
        check_vma=False,
    )
```

```python
import functools
import math

import jax
import jax.numpy as jnp
from jax import lax
from jax.experimental import pallas as pl
from jax.experimental.pallas import tpu as pltpu
from jax.sharding import PartitionSpec as P

HEADS = 8
HD = 64
REACH = 2
TAPS = 72
DEEP = 256
NEG_FILL = -1e30
MIB = 1024 * 1024


def nt_dot(a, b):
    return lax.dot_general(a, b, (((1,), (1,)), ((), ())), preferred_element_type=jnp.float32)


def high(x):
    return x.astype(jnp.bfloat16).astype(jnp.float32)


def split_lanes(x):
    lane = lax.broadcasted_iota(jnp.int32, x.shape, 1)
    first = high(x)
    rest = x - first
    second = high(rest)
    third = rest - second
    return jnp.where(lane < TAPS, first, jnp.where(lane < 2 * TAPS, second, third)).astype(
        jnp.bfloat16
    )


def flat_taps(ref):
    rows = [ref[i, j].astype(jnp.float32) for i in range(3) for j in range(3)]
    return jnp.concatenate(rows, axis=0)


def prepare_kernel(
    views, edges_hbm, conv_in_hbm, conv_out_hbm, wq_hbm, wkv_hbm,
    gc, mq, mk, taps, bias, edges_ref, conv_in, conv_out, wq, wk, sems,
):
    parts = (
        (edges_hbm, edges_ref),
        (conv_in_hbm, conv_in),
        (wq_hbm, wq),
        (wkv_hbm.at[:, : HEADS * HD], wk),
        (conv_out_hbm, conv_out),
    )
    copies = [pltpu.make_async_copy(src, dst, sems.at[n]) for n, (src, dst) in enumerate(parts)]
    for copy in copies:
        copy.start()
    local = bias.shape[0]
    span = bias.shape[1]
    total = views * local
    first = lax.axis_index("view") * local
    copies[0].wait()
    source = edges_ref[0:1, :]
    target = edges_ref[1:2, :]
    slot = lax.broadcasted_iota(jnp.int32, (span, 1), 0)
    near = first - REACH + slot
    near = jnp.where(near < 0, near + total, near)
    near = jnp.where(near >= total, near - total, near)
    for v in range(local):
        own = first + v
        hit = ((source == own) & (target == near)) | ((target == own) & (source == near))
        linked = jnp.max(hit.astype(jnp.float32), axis=1, keepdims=True)
        linked = jnp.where(slot == v + REACH, 1.0, linked)
        inside = (slot >= v) & (slot <= v + 2 * REACH)
        allowed = (linked > 0.5) & inside
        bias[v] = jnp.broadcast_to(jnp.where(allowed, 0.0, NEG_FILL), bias.shape[1:])
    copies[1].wait()
    wc = flat_taps(conv_in)
    wcb = wc.astype(jnp.bfloat16)
    copies[2].wait()
    mq[...] = jnp.dot(wcb, wq[...], preferred_element_type=jnp.float32)
    copies[3].wait()
    mk[...] = jnp.dot(wcb, wk[...], preferred_element_type=jnp.float32)
    copies[4].wait()
    wt = flat_taps(conv_out)
    pad = jnp.zeros((DEEP - 3 * TAPS, wc.shape[1]), jnp.float32)
    wc3 = jnp.concatenate([wc, wc, wc, pad], axis=0).astype(jnp.bfloat16)
    taps[...] = jnp.concatenate([wc, wt], axis=0).astype(jnp.bfloat16)
    gc[...] = split_lanes(nt_dot(taps[...], wc3))


def nt_dot_parts(a, b):
    ah, bh = high(a), high(b)
    left = jnp.concatenate([ah, a - ah, ah], axis=1).astype(jnp.bfloat16)
    right = jnp.concatenate([bh, bh, b - bh], axis=1).astype(jnp.bfloat16)
    return nt_dot(left, right)


def head_pair(g):
    lane = lax.broadcasted_iota(jnp.int32, (TAPS, 2 * HD), 1)
    even = (lane < HD).astype(jnp.float32)
    return slice(g * 2 * HD, (g + 1) * 2 * HD), even, 1.0 - even


def score_products(mq, mk, aq):
    pad = jnp.zeros((DEEP - 3 * TAPS, 2 * HD), jnp.float32)
    scale = math.log2(math.e) / math.sqrt(HD)
    for g in range(HEADS // 2):
        cols, even, odd = head_pair(g)
        q = mq[:, cols] * scale
        k = mk[:, cols]
        q3 = jnp.concatenate([q, q, q, pad], axis=0)
        k2 = jnp.concatenate([k * even, k * odd], axis=0)
        aq[(g + 1) * 2 * TAPS : (g + 2) * 2 * TAPS, :] = split_lanes(nt_dot_parts(k2, q3))


def value_products(mv, nt, bb):
    for g in range(HEADS // 2):
        cols, even, odd = head_pair(g)
        v = mv[:, cols]
        v2 = jnp.concatenate([v * even, v * odd], axis=0)
        b = nt_dot_parts(nt[:, cols], v2)
        bh = high(b)
        bb[g] = jnp.concatenate([bh, b - bh], axis=0).astype(jnp.bfloat16)


def shifted(x, by):
    lane = lax.broadcasted_iota(jnp.int32, x.shape, x.ndim - 1)
    width = x.shape[-1]
    if by == 1:
        return jnp.where(lane == 0, 0.0, pltpu.roll(x, 1, x.ndim - 1))
    return jnp.where(lane == width - 1, 0.0, pltpu.roll(x, width - 1, x.ndim - 1))


def is_even(axis):
    return lax.rem(lax.axis_index(axis), 2) == 0


def pack_kernel(own, first, second, after, rows, tail, lead):
    local = own.shape[0]
    even = is_even("space")
    kind = own.dtype
    for v in range(local):
        one = first[v].astype(jnp.float32)
        two = second[v].astype(jnp.float32)
        rows[v, 0] = jnp.where(even, two, one).astype(kind)
        rows[v, 1] = own[v]
        rows[v, 2] = jnp.where(even, one, two).astype(kind)
    for n in range(REACH):
        for i in range(3):
            tail[n, i] = rows[local - REACH + n, i]
            lead[n, i] = rows[n, i]


def patch_stack(rows):
    parts = []
    for row in rows:
        row = row.astype(jnp.float32)
        parts += [shifted(row, 1), row, shifted(row, -1)]
    patch = jnp.concatenate(parts, axis=0)
    pad = jnp.zeros((DEEP - 3 * TAPS, patch.shape[1]), jnp.float32)
    return jnp.concatenate([patch, patch, patch, pad], axis=0).astype(jnp.bfloat16)


def token_rate(gram_patches, patches):
    square = jnp.sum(gram_patches * patches, axis=0, keepdims=True) * (1.0 / 1024)
    return lax.rsqrt(jnp.maximum(square, 0.0) + 1e-6)


def store_keys(keyed, slots, kl, vl):
    w = keyed.shape[1] // len(slots)
    kh = high(keyed)
    low = keyed - kh
    sub = lax.broadcasted_iota(jnp.int32, (8, w), 0)
    for n, u in enumerate(slots):
        cols = slice(n * w, (n + 1) * w)
        onehot = (sub == u).astype(jnp.float32)
        h = kh[:, cols]
        r = low[:, cols]
        vl[:, cols] = jnp.concatenate([h, jnp.ones((8, w), jnp.float32), r], axis=0).astype(
            jnp.bfloat16
        )
        tall = jnp.concatenate(
            [h, onehot, r, h, jnp.zeros((DEEP - 3 * TAPS - 8, w), jnp.float32)], axis=0
        )
        kl[cols, :] = tall.T.astype(jnp.bfloat16)


def own_kernel(
    rows, gc, mq, mk, taps, bias, wkv_hbm, wo_hbm,
    qr, skip, bb, top, acc, p3, aq, kl, vl, sc, ex, wv, wo, sems,
):
    local, _, _, w = rows.shape
    copies = [
        pltpu.make_async_copy(wkv_hbm.at[:, HEADS * HD :], wv, sems.at[0]),
        pltpu.make_async_copy(wo_hbm, wo, sems.at[1]),
    ]
    for copy in copies:
        copy.start()
    aq[0 : 2 * TAPS, :] = gc[...]
    score_products(mq, mk, aq)
    for v in range(local):
        p3[:, v * w : (v + 1) * w] = patch_stack([rows[v, i] for i in range(3)])
    asked = jnp.dot(aq[...], p3[...], preferred_element_type=jnp.float32)
    patches = p3[0:TAPS, :].astype(jnp.float32)
    rate = token_rate(asked[0:TAPS], patches)
    skip[...] = asked[TAPS : 2 * TAPS]
    store_keys(patches * rate, range(REACH, REACH + local), kl, vl)
    for v in range(local):
        for head in range(HEADS):
            q = asked[(head + 2) * TAPS : (head + 3) * TAPS, v * w : (v + 1) * w]
            q = q * rate[:, v * w : (v + 1) * w]
            h = high(q)
            qr[v, :, head * w : (head + 1) * w] = jnp.concatenate(
                [h, bias[v], h, q - h, jnp.zeros((DEEP - 3 * TAPS - 8, w), jnp.float32)], axis=0
            ).astype(jnp.bfloat16)
    spans = [(max(v - REACH, 0) * w, min(v + REACH + 1, local) * w) for v in range(local)]

    def scored(v):
        lo, hi = spans[v]
        sc[v % 2, 0 : hi - lo, :] = jnp.dot(
            kl[lo:hi, :], qr[v], preferred_element_type=jnp.float32
        )

    scored(0)
    for v in range(local):
        if v + 1 < local:
            scored(v + 1)
        if v == local // 2:
            copies[0].wait()
            copies[1].wait()
            mv = jnp.dot(taps[0:TAPS, :], wv[...], preferred_element_type=jnp.float32)
            value_products(mv, nt_dot(taps[TAPS:, :], wo[...]), bb)
        lo, hi = spans[v]
        for head in range(HEADS):
            cols = slice(head * w, (head + 1) * w)
            scores = sc[v % 2, 0 : hi - lo, cols]
            largest = jnp.max(scores, axis=0, keepdims=True)
            top[v : v + 1, cols] = largest
            ex[v % 2, 0 : hi - lo, cols] = jnp.exp2(scores - largest).astype(jnp.bfloat16)
        gathered = jnp.dot(
            vl[:, lo:hi], ex[v % 2, 0 : hi - lo, :], preferred_element_type=jnp.float32
        )
        acc[v, 0:TAPS, :] = gathered[0:TAPS] + gathered[TAPS + 8 :]
        acc[v, TAPS:, :] = gathered[TAPS : TAPS + 8]

def mix_kernel(
    prev, nxt, gc, bb, qr, skip, top, acc,
    mine, late, early, p3, kl, vl, sc, ex,
):
    local, _, w = mine.shape
    even = is_even("space")
    for u in range(REACH):
        p3[:, u * w : (u + 1) * w] = patch_stack([prev[u, i] for i in range(3)])
        p3[:, (REACH + u) * w : (REACH + u + 1) * w] = patch_stack([nxt[u, i] for i in range(3)])
    gram = jnp.dot(gc[0:TAPS, :], p3[...], preferred_element_type=jnp.float32)
    patches = p3[0:TAPS, :].astype(jnp.float32)
    rate = token_rate(gram, patches)
    slots = [*range(REACH), *range(REACH + local, 2 * REACH + local)]
    store_keys(patches * rate, slots, kl, vl)
    spans = []
    for v in range(local):
        near = [n for n, u in enumerate(slots) if v <= u <= v + 2 * REACH]
        spans.append((near[0] * w, (near[-1] + 1) * w))
    for v, (lo, hi) in enumerate(spans):
        sc[v, 0 : hi - lo, :] = jnp.dot(
            kl[lo:hi, :], qr[v], preferred_element_type=jnp.float32
        )
    for v in sorted(range(local), key=lambda v: spans[v][0] - spans[v][1]):
        lo, hi = spans[v]
        fades = []
        for head in range(HEADS):
            cols = slice(head * w, (head + 1) * w)
            scores = sc[v, 0 : hi - lo, cols]
            before = top[v : v + 1, cols]
            largest = jnp.maximum(jnp.max(scores, axis=0, keepdims=True), before)
            fades.append(jnp.exp2(before - largest))
            ex[v, 0 : hi - lo, cols] = jnp.exp2(scores - largest).astype(jnp.bfloat16)
        fade = jnp.concatenate(fades, axis=1)
        gathered = jnp.dot(
            vl[:, lo:hi], ex[v, 0 : hi - lo, :], preferred_element_type=jnp.float32
        )
        weight = gathered[TAPS : TAPS + 1] + acc[v, TAPS : TAPS + 1, :] * fade
        mixed = gathered[0:TAPS] + gathered[TAPS + 8 :] + acc[v, 0:TAPS, :] * fade
        mixed = mixed * (1.0 / weight)
        z = skip[:, v * w : (v + 1) * w]
        for g in range(HEADS // 2):
            pair = mixed[:, g * 2 * w : (g + 1) * 2 * w]
            pair = jnp.concatenate([pair[:, :w], pair[:, w:]], axis=0)
            h = pair.astype(jnp.bfloat16)
            r = (pair - h.astype(jnp.float32)).astype(jnp.bfloat16)
            y = jnp.dot(bb[g], h, preferred_element_type=jnp.float32)
            z = z + y[:TAPS] + y[TAPS:]
            z = z + jnp.dot(bb[g, 0:TAPS, :], r, preferred_element_type=jnp.float32)
        parts = []
        for i in range(3):
            rows = z[i * 24 : (i + 1) * 24]
            parts.append(shifted(rows[0:8], 1) + rows[8:16] + shifted(rows[16:24], -1))
        below, mine[v], above = parts
        early[v] = jnp.where(even, below, above)
        late[v] = jnp.where(even, above, below)


def pairs(count, start):
    both = []
    for i in range(start, count - 1, 2):
        both += [(i, i + 1), (i + 1, i)]
    return both


def on_device(
    latent,
    camera_edges,
    conv_in_weight,
    query_weight,
    key_value_weight,
    out_weight,
    conv_out_weight,
):
    local, channels, _, w = latent.shape
    span = local + 2 * REACH
    views = lax.axis_size("view")
    space = lax.axis_size("space")
    x = latent.reshape(local, channels, w)
    row_first = lax.ppermute(x, "space", pairs(space, 0))
    row_second = lax.ppermute(x, "space", pairs(space, 1))

    f32, bf16 = jnp.float32, jnp.bfloat16
    whole = pl.BlockSpec(memory_space=pltpu.VMEM)
    far = pl.BlockSpec(memory_space=pltpu.HBM)
    loaded = (
        camera_edges.T,
        conv_in_weight,
        conv_out_weight,
        query_weight,
        key_value_weight,
    )
    gc, mq, mk, taps, bias = pl.pallas_call(
        functools.partial(prepare_kernel, views),
        in_specs=[far] * len(loaded),
        out_specs=[whole] * 5,
        out_shape=[
            pltpu.VMEM((2 * TAPS, DEEP), bf16),
            pltpu.VMEM((TAPS, HEADS * HD), f32),
            pltpu.VMEM((TAPS, HEADS * HD), f32),
            pltpu.VMEM((2 * TAPS, out_weight.shape[1]), bf16),
            pltpu.VMEM((local, span, w), f32),
        ],
        scratch_shapes=[
            pltpu.VMEM(a.shape, a.dtype)
            for a in (*loaded[:4], query_weight)
        ]
        + [pltpu.SemaphoreType.DMA((5,))],
        compiler_params=pltpu.CompilerParams(vmem_limit_bytes=60 * MIB),
        cost_estimate=pl.CostEstimate(
            flops=3_000_000_000, bytes_accessed=5_000_000, transcendentals=0
        ),
    )(*loaded)

    part = jax.ShapeDtypeStruct((REACH, 3, channels, w), bf16)
    rows, tail, lead = pl.pallas_call(
        pack_kernel,
        in_specs=[whole] * 3 + [pl.BlockSpec(memory_space=pl.ANY)],
        out_specs=[whole] * 3,
        out_shape=[pltpu.VMEM((local, 3, channels, w), bf16), part, part],
        compiler_params=pltpu.CompilerParams(vmem_limit_bytes=4 * MIB),
    )(x, row_first, row_second, bias)
    prev = lax.ppermute(tail, "view", [(i, (i + 1) % views) for i in range(views)])
    nxt = lax.ppermute(lead, "view", [((i + 1) % views, i) for i in range(views)])

    keys_scratch = [
        pltpu.VMEM((local * w, DEEP), bf16),
        pltpu.VMEM((2 * TAPS + 8, local * w), bf16),
    ]
    qr, skip, bb, top, acc = pl.pallas_call(
        own_kernel,
        in_specs=[whole] * 6 + [far] * 2,
        out_specs=[whole] * 5,
        out_shape=[
            pltpu.VMEM((local, DEEP, HEADS * w), bf16),
            pltpu.VMEM((TAPS, local * w), f32),
            pltpu.VMEM((HEADS // 2, 2 * TAPS, 2 * TAPS), bf16),
            pltpu.VMEM((local, HEADS * w), f32),
            pltpu.VMEM((local, TAPS + 8, HEADS * w), f32),
        ],
        scratch_shapes=[
            pltpu.VMEM((DEEP, local * w), bf16),
            pltpu.VMEM(((HEADS + 2) * TAPS, DEEP), bf16),
            *keys_scratch,
            pltpu.VMEM((2, local * w, HEADS * w), f32),
            pltpu.VMEM((2, local * w, HEADS * w), bf16),
            pltpu.VMEM(query_weight.shape, bf16),
            pltpu.VMEM(out_weight.shape, bf16),
            pltpu.SemaphoreType.DMA((2,)),
        ],
        compiler_params=pltpu.CompilerParams(vmem_limit_bytes=49 * MIB),
        cost_estimate=pl.CostEstimate(
            flops=4_000_000_000, bytes_accessed=1_000_000, transcendentals=2_000_000
        ),
    )(rows, gc, mq, mk, taps, bias, key_value_weight, out_weight)

    plane = jax.ShapeDtypeStruct((local, channels, w), f32)
    mine, late, early = pl.pallas_call(
        mix_kernel,
        in_specs=[whole] * 8,
        out_specs=[whole] * 3,
        out_shape=[plane] * 3,
        scratch_shapes=[
            pltpu.VMEM((DEEP, 2 * REACH * w), bf16),
            *keys_scratch,
            pltpu.VMEM((local, REACH * w, HEADS * w), f32),
            pltpu.VMEM((local, REACH * w, HEADS * w), bf16),
        ],
        compiler_params=pltpu.CompilerParams(vmem_limit_bytes=24 * MIB),
        cost_estimate=pl.CostEstimate(
            flops=3_000_000_000, bytes_accessed=1_000_000, transcendentals=1_000_000
        ),
    )(prev, nxt, gc, bb, qr, skip, top, acc)

    row_second = lax.ppermute(late, "space", pairs(space, 1))
    row_first = lax.ppermute(early, "space", pairs(space, 0))
    return (row_second + mine + row_first).reshape(local, channels, 1, w)


def solution(mesh):
    placed = (P("view", None, "space", None), P(), P(), P(), P(), P(), P())
    return jax.shard_map(
        on_device,
        mesh=mesh,
        in_specs=placed,
        out_specs=P("view", None, "space", None),
        check_vma=False,
    )
```

```python
import functools
import math

import jax
import jax.numpy as jnp
from jax import lax
from jax.experimental import pallas as pl
from jax.experimental.pallas import tpu as pltpu
from jax.sharding import PartitionSpec as P

HEADS = 8
HD = 64
REACH = 2
TAPS = 72
DEEP = 256
NEG_FILL = -1e30
MIB = 1024 * 1024


def nt_dot(a, b):
    return lax.dot_general(a, b, (((1,), (1,)), ((), ())), preferred_element_type=jnp.float32)


def high(x):
    return x.astype(jnp.bfloat16).astype(jnp.float32)


def split_lanes(x):
    lane = lax.broadcasted_iota(jnp.int32, x.shape, 1)
    first = high(x)
    rest = x - first
    second = high(rest)
    third = rest - second
    return jnp.where(lane < TAPS, first, jnp.where(lane < 2 * TAPS, second, third)).astype(
        jnp.bfloat16
    )


def flat_taps(ref):
    rows = [ref[i, j].astype(jnp.float32) for i in range(3) for j in range(3)]
    return jnp.concatenate(rows, axis=0)


def prepare_kernel(
    views, edges_hbm, conv_in_hbm, conv_out_hbm, wq_hbm, wkv_hbm,
    gc, mq, mkv, wt, bias, edges_ref, conv_in, conv_out, wq, wk, wv, sems,
):
    wide = HEADS * HD
    keys, values = slice(0, wide), slice(wide, 2 * wide)
    parts = (
        (edges_hbm, edges_ref),
        (conv_in_hbm, conv_in),
        (wq_hbm, wq),
        (wkv_hbm.at[:, keys], wk),
        (conv_out_hbm, conv_out),
        (wkv_hbm.at[:, values], wv),
    )
    copies = [pltpu.make_async_copy(src, dst, sems.at[n]) for n, (src, dst) in enumerate(parts)]
    for copy in copies:
        copy.start()
    local = bias.shape[0]
    span = bias.shape[1]
    total = views * local
    first = lax.axis_index("view") * local
    copies[0].wait()
    source = edges_ref[0:1, :]
    target = edges_ref[1:2, :]
    slot = lax.broadcasted_iota(jnp.int32, (span, 1), 0)
    near = first - REACH + slot
    near = jnp.where(near < 0, near + total, near)
    near = jnp.where(near >= total, near - total, near)
    for v in range(local):
        own = first + v
        hit = ((source == own) & (target == near)) | ((target == own) & (source == near))
        linked = jnp.max(hit.astype(jnp.float32), axis=1, keepdims=True)
        linked = jnp.where(slot == v + REACH, 1.0, linked)
        inside = (slot >= v) & (slot <= v + 2 * REACH)
        allowed = (linked > 0.5) & inside
        bias[v] = jnp.broadcast_to(jnp.where(allowed, 0.0, NEG_FILL), bias.shape[1:])
    copies[1].wait()
    wc = flat_taps(conv_in)
    wcb = wc.astype(jnp.bfloat16)
    copies[2].wait()
    mq[...] = jnp.dot(wcb, wq[...], preferred_element_type=jnp.float32)
    copies[3].wait()
    mkv[:, keys] = jnp.dot(wcb, wk[...], preferred_element_type=jnp.float32)
    copies[4].wait()
    taps = flat_taps(conv_out)
    wt[...] = taps.astype(jnp.bfloat16)
    pad = jnp.zeros((DEEP - 3 * TAPS, wc.shape[1]), jnp.float32)
    wc3 = jnp.concatenate([wc, wc, wc, pad], axis=0).astype(jnp.bfloat16)
    both = jnp.concatenate([wc, taps], axis=0).astype(jnp.bfloat16)
    gc[...] = split_lanes(nt_dot(both, wc3))
    copies[5].wait()
    mkv[:, values] = jnp.dot(wcb, wv[...], preferred_element_type=jnp.float32)


def nt_dot_parts(a, b):
    ah, bh = high(a), high(b)
    left = jnp.concatenate([ah, a - ah, ah], axis=1).astype(jnp.bfloat16)
    right = jnp.concatenate([bh, bh, b - bh], axis=1).astype(jnp.bfloat16)
    return nt_dot(left, right)


def head_pair(g):
    lane = lax.broadcasted_iota(jnp.int32, (TAPS, 2 * HD), 1)
    even = (lane < HD).astype(jnp.float32)
    return slice(g * 2 * HD, (g + 1) * 2 * HD), even, 1.0 - even


def score_products(mq, mk, aq):
    scale = math.log2(math.e) / math.sqrt(HD)
    lane = lax.broadcasted_iota(jnp.int32, (2 * TAPS, 2 * TAPS), 1)
    for g in range(HEADS // 2):
        cols, even, odd = head_pair(g)
        q = mq[:, cols] * scale
        k = mk[:, cols]
        q2 = jnp.concatenate([q, q], axis=0)
        k2 = jnp.concatenate([k * even, k * odd], axis=0)
        a = nt_dot_parts(k2, q2)
        ah = high(a)
        aq[g * 2 * TAPS : (g + 1) * 2 * TAPS, :] = jnp.where(lane < TAPS, ah, a - ah).astype(
            jnp.bfloat16
        )


def value_products(mkv, nt, bb):
    for g in range(HEADS // 2):
        cols, even, odd = head_pair(g)
        v = mkv[:, cols.start + HEADS * HD : cols.stop + HEADS * HD]
        v2 = jnp.concatenate([v * even, v * odd], axis=0)
        b = nt_dot_parts(nt[:, cols], v2)
        bh = high(b)
        bb[g] = jnp.concatenate([bh, b - bh], axis=0).astype(jnp.bfloat16)


def shifted(x, by):
    lane = lax.broadcasted_iota(jnp.int32, x.shape, x.ndim - 1)
    width = x.shape[-1]
    if by == 1:
        return jnp.where(lane == 0, 0.0, pltpu.roll(x, 1, x.ndim - 1))
    return jnp.where(lane == width - 1, 0.0, pltpu.roll(x, width - 1, x.ndim - 1))


def is_even(axis):
    return lax.rem(lax.axis_index(axis), 2) == 0


def pack_kernel(own, first, second, after, rows, tail, lead):
    local = own.shape[0]
    even = is_even("space")
    kind = own.dtype
    for v in range(local):
        one = first[v].astype(jnp.float32)
        two = second[v].astype(jnp.float32)
        rows[v, 0] = jnp.where(even, two, one).astype(kind)
        rows[v, 1] = own[v]
        rows[v, 2] = jnp.where(even, one, two).astype(kind)
    for n in range(REACH):
        for i in range(3):
            tail[n, i] = rows[local - REACH + n, i]
            lead[n, i] = rows[n, i]


def patch_stack(rows):
    parts = []
    for row in rows:
        row = row.astype(jnp.float32)
        parts += [shifted(row, 1), row, shifted(row, -1)]
    patch = jnp.concatenate(parts, axis=0)
    pad = jnp.zeros((DEEP - 3 * TAPS, patch.shape[1]), jnp.float32)
    return jnp.concatenate([patch, patch, patch, pad], axis=0).astype(jnp.bfloat16)


def token_rate(gram_patches, patches):
    square = jnp.sum(gram_patches * patches, axis=0, keepdims=True) * (1.0 / 1024)
    return lax.rsqrt(jnp.maximum(square, 0.0) + 1e-6)


def store_keys(keyed, slots, kl, vl):
    w = keyed.shape[1] // len(slots)
    kh = high(keyed)
    low = keyed - kh
    sub = lax.broadcasted_iota(jnp.int32, (8, w), 0)
    for n, u in enumerate(slots):
        cols = slice(n * w, (n + 1) * w)
        onehot = (sub == u).astype(jnp.float32)
        h = kh[:, cols]
        r = low[:, cols]
        vl[:, cols] = jnp.concatenate([h, jnp.ones((8, w), jnp.float32), r], axis=0).astype(
            jnp.bfloat16
        )
        tall = jnp.concatenate(
            [h, onehot, r, h, jnp.zeros((DEEP - 3 * TAPS - 8, w), jnp.float32)], axis=0
        )
        kl[cols, :] = tall.T.astype(jnp.bfloat16)


def own_kernel(
    rows, gc, mq, mkv, wt, bias, wo_hbm,
    qr, skip, bb, top, acc, p3, aq, kl, vl, sc, ex, wo, sem,
):
    local, _, _, w = rows.shape
    copy = pltpu.make_async_copy(wo_hbm, wo, sem)
    copy.start()
    score_products(mq, mkv, aq)
    for v in range(local):
        p3[:, v * w : (v + 1) * w] = patch_stack([rows[v, i] for i in range(3)])
    base = jnp.dot(gc[...], p3[...], preferred_element_type=jnp.float32)
    asked = jnp.dot(aq[...], p3[0 : 2 * TAPS, :], preferred_element_type=jnp.float32)
    patches = p3[0:TAPS, :].astype(jnp.float32)
    rate = token_rate(base[0:TAPS], patches)
    skip[...] = base[TAPS:]
    store_keys(patches * rate, range(REACH, REACH + local), kl, vl)
    for v in range(local):
        for head in range(HEADS):
            q = asked[head * TAPS : (head + 1) * TAPS, v * w : (v + 1) * w]
            q = q * rate[:, v * w : (v + 1) * w]
            h = high(q)
            qr[v, :, head * w : (head + 1) * w] = jnp.concatenate(
                [h, bias[v], h, q - h, jnp.zeros((DEEP - 3 * TAPS - 8, w), jnp.float32)], axis=0
            ).astype(jnp.bfloat16)
    spans = [(max(v - REACH, 0) * w, min(v + REACH + 1, local) * w) for v in range(local)]

    def scored(v):
        lo, hi = spans[v]
        sc[v % 2, 0 : hi - lo, :] = jnp.dot(
            kl[lo:hi, :], qr[v], preferred_element_type=jnp.float32
        )

    scored(0)
    for v in range(local):
        if v + 1 < local:
            scored(v + 1)
        lo, hi = spans[v]
        for head in range(HEADS):
            cols = slice(head * w, (head + 1) * w)
            scores = sc[v % 2, 0 : hi - lo, cols]
            largest = jnp.max(scores, axis=0, keepdims=True)
            top[v : v + 1, cols] = largest
            ex[v % 2, 0 : hi - lo, cols] = jnp.exp2((scores - largest).astype(jnp.bfloat16))
        gathered = jnp.dot(
            vl[:, lo:hi], ex[v % 2, 0 : hi - lo, :], preferred_element_type=jnp.float32
        )
        acc[v, 0:TAPS, :] = gathered[0:TAPS] + gathered[TAPS + 8 :]
        acc[v, TAPS:, :] = gathered[TAPS : TAPS + 8]
    copy.wait()
    value_products(mkv, nt_dot(wt[...], wo[...]), bb)


def mix_kernel(
    prev, nxt, gc, bb, qr, skip, top, acc,
    mine, late, early, p3, kl, vl, uh, ul, sc, ex,
):
    local, _, w = mine.shape
    for u in range(REACH):
        p3[:, u * w : (u + 1) * w] = patch_stack([prev[u, i] for i in range(3)])
        p3[:, (REACH + u) * w : (REACH + u + 1) * w] = patch_stack([nxt[u, i] for i in range(3)])
    gram = jnp.dot(gc[0:TAPS, :], p3[...], preferred_element_type=jnp.float32)
    patches = p3[0:TAPS, :].astype(jnp.float32)
    rate = token_rate(gram, patches)
    slots = [*range(REACH), *range(REACH + local, 2 * REACH + local)]
    store_keys(patches * rate, slots, kl, vl)
    spans = []
    for v in range(local):
        near = [n for n, u in enumerate(slots) if v <= u <= v + 2 * REACH]
        spans.append((near[0] * w, (near[-1] + 1) * w))
    for v, (lo, hi) in enumerate(spans):
        sc[v, 0 : hi - lo, :] = jnp.dot(
            kl[lo:hi, :], qr[v], preferred_element_type=jnp.float32
        )
    for v, (lo, hi) in enumerate(spans):
        fades = []
        for head in range(HEADS):
            cols = slice(head * w, (head + 1) * w)
            scores = sc[v, 0 : hi - lo, cols]
            before = top[v : v + 1, cols]
            largest = jnp.maximum(jnp.max(scores, axis=0, keepdims=True), before)
            fades.append(jnp.exp2(before - largest))
            ex[v, 0 : hi - lo, cols] = jnp.exp2((scores - largest).astype(jnp.bfloat16))
        fade = jnp.concatenate(fades, axis=1)
        gathered = jnp.dot(
            vl[:, lo:hi], ex[v, 0 : hi - lo, :], preferred_element_type=jnp.float32
        )
        weight = gathered[TAPS : TAPS + 1] + acc[v, TAPS : TAPS + 1, :] * fade
        mixed = gathered[0:TAPS] + gathered[TAPS + 8 :] + acc[v, 0:TAPS, :] * fade
        mixed = mixed * (1.0 / weight)
        for g in range(HEADS // 2):
            pair = mixed[:, g * 2 * w : (g + 1) * 2 * w]
            pair = jnp.concatenate([pair[:, :w], pair[:, w:]], axis=0)
            h = pair.astype(jnp.bfloat16)
            uh[g, :, v * w : (v + 1) * w] = h
            ul[g, :, v * w : (v + 1) * w] = (pair - h.astype(jnp.float32)).astype(jnp.bfloat16)
    z = skip[...]
    for g in range(HEADS // 2):
        y = jnp.dot(bb[g], uh[g], preferred_element_type=jnp.float32)
        z = z + y[:TAPS] + y[TAPS:]
        z = z + jnp.dot(bb[g, 0:TAPS, :], ul[g], preferred_element_type=jnp.float32)
    even = is_even("space")
    for v in range(local):
        parts = []
        for i in range(3):
            rows = z[i * 24 : (i + 1) * 24, v * w : (v + 1) * w]
            parts.append(shifted(rows[0:8], 1) + rows[8:16] + shifted(rows[16:24], -1))
        below, mine[v], above = parts
        early[v] = jnp.where(even, below, above)
        late[v] = jnp.where(even, above, below)


def pairs(count, start):
    both = []
    for i in range(start, count - 1, 2):
        both += [(i, i + 1), (i + 1, i)]
    return both


def on_device(
    latent,
    camera_edges,
    conv_in_weight,
    query_weight,
    key_value_weight,
    out_weight,
    conv_out_weight,
):
    local, channels, _, w = latent.shape
    span = local + 2 * REACH
    views = lax.axis_size("view")
    space = lax.axis_size("space")
    x = latent.reshape(local, channels, w)
    row_first = lax.ppermute(x, "space", pairs(space, 0))
    row_second = lax.ppermute(x, "space", pairs(space, 1))

    f32, bf16 = jnp.float32, jnp.bfloat16
    whole = pl.BlockSpec(memory_space=pltpu.VMEM)
    far = pl.BlockSpec(memory_space=pltpu.HBM)
    loaded = (
        camera_edges.T,
        conv_in_weight,
        conv_out_weight,
        query_weight,
        key_value_weight,
    )
    gc, mq, mkv, wt, bias = pl.pallas_call(
        functools.partial(prepare_kernel, views),
        in_specs=[far] * len(loaded),
        out_specs=[whole] * 5,
        out_shape=[
            pltpu.VMEM((2 * TAPS, DEEP), bf16),
            pltpu.VMEM((TAPS, HEADS * HD), f32),
            pltpu.VMEM((TAPS, 2 * HEADS * HD), f32),
            pltpu.VMEM((TAPS, out_weight.shape[1]), bf16),
            pltpu.VMEM((local, span, w), f32),
        ],
        scratch_shapes=[
            pltpu.VMEM(a.shape, a.dtype)
            for a in (*loaded[:4], query_weight, query_weight)
        ]
        + [pltpu.SemaphoreType.DMA((6,))],
        compiler_params=pltpu.CompilerParams(vmem_limit_bytes=60 * MIB),
        cost_estimate=pl.CostEstimate(
            flops=3_000_000_000, bytes_accessed=5_000_000, transcendentals=0
        ),
    )(*loaded)

    part = jax.ShapeDtypeStruct((REACH, 3, channels, w), bf16)
    rows, tail, lead = pl.pallas_call(
        pack_kernel,
        in_specs=[whole] * 3 + [pl.BlockSpec(memory_space=pl.ANY)],
        out_specs=[whole] * 3,
        out_shape=[pltpu.VMEM((local, 3, channels, w), bf16), part, part],
        compiler_params=pltpu.CompilerParams(vmem_limit_bytes=4 * MIB),
    )(x, row_first, row_second, bias)
    prev = lax.ppermute(tail, "view", [(i, (i + 1) % views) for i in range(views)])
    nxt = lax.ppermute(lead, "view", [((i + 1) % views, i) for i in range(views)])

    keys_scratch = [
        pltpu.VMEM((local * w, DEEP), bf16),
        pltpu.VMEM((2 * TAPS + 8, local * w), bf16),
    ]
    qr, skip, bb, top, acc = pl.pallas_call(
        own_kernel,
        in_specs=[whole] * 6 + [far],
        out_specs=[whole] * 5,
        out_shape=[
            pltpu.VMEM((local, DEEP, HEADS * w), bf16),
            pltpu.VMEM((TAPS, local * w), f32),
            pltpu.VMEM((HEADS // 2, 2 * TAPS, 2 * TAPS), bf16),
            pltpu.VMEM((local, HEADS * w), f32),
            pltpu.VMEM((local, TAPS + 8, HEADS * w), f32),
        ],
        scratch_shapes=[
            pltpu.VMEM((DEEP, local * w), bf16),
            pltpu.VMEM((HEADS * TAPS, 2 * TAPS), bf16),
            *keys_scratch,
            pltpu.VMEM((2, local * w, HEADS * w), f32),
            pltpu.VMEM((2, local * w, HEADS * w), bf16),
            pltpu.VMEM(out_weight.shape, bf16),
            pltpu.SemaphoreType.DMA,
        ],
        compiler_params=pltpu.CompilerParams(vmem_limit_bytes=49 * MIB),
        cost_estimate=pl.CostEstimate(
            flops=4_000_000_000, bytes_accessed=1_000_000, transcendentals=2_000_000
        ),
    )(rows, gc, mq, mkv, wt, bias, out_weight)

    plane = jax.ShapeDtypeStruct((local, channels, w), f32)
    mine, late, early = pl.pallas_call(
        mix_kernel,
        in_specs=[whole] * 8,
        out_specs=[whole] * 3,
        out_shape=[plane] * 3,
        scratch_shapes=[
            pltpu.VMEM((DEEP, 2 * REACH * w), bf16),
            *keys_scratch,
            pltpu.VMEM((HEADS // 2, 2 * TAPS, local * w), bf16),
            pltpu.VMEM((HEADS // 2, 2 * TAPS, local * w), bf16),
            pltpu.VMEM((local, REACH * w, HEADS * w), f32),
            pltpu.VMEM((local, REACH * w, HEADS * w), bf16),
        ],
        compiler_params=pltpu.CompilerParams(vmem_limit_bytes=24 * MIB),
        cost_estimate=pl.CostEstimate(
            flops=3_000_000_000, bytes_accessed=1_000_000, transcendentals=1_000_000
        ),
    )(prev, nxt, gc, bb, qr, skip, top, acc)

    row_second = lax.ppermute(late, "space", pairs(space, 1))
    row_first = lax.ppermute(early, "space", pairs(space, 0))
    return (row_second + mine + row_first).reshape(local, channels, 1, w)


def solution(mesh):
    placed = (P("view", None, "space", None), P(), P(), P(), P(), P(), P())
    return jax.shard_map(
        on_device,
        mesh=mesh,
        in_specs=placed,
        out_specs=P("view", None, "space", None),
        check_vma=False,
    )
```

```python
import functools
import math

import jax
import jax.numpy as jnp
from jax import lax
from jax.experimental import pallas as pl
from jax.experimental.pallas import tpu as pltpu
from jax.sharding import PartitionSpec as P

HEADS = 8
HD = 64
REACH = 2
TAPS = 72
DEEP = 256
NEG_FILL = -1e30
MIB = 1024 * 1024


def nt_dot(a, b):
    return lax.dot_general(a, b, (((1,), (1,)), ((), ())), preferred_element_type=jnp.float32)


def high(x):
    return x.astype(jnp.bfloat16).astype(jnp.float32)


def split_lanes(x):
    lane = lax.broadcasted_iota(jnp.int32, x.shape, 1)
    first = high(x)
    rest = x - first
    second = high(rest)
    third = rest - second
    return jnp.where(lane < TAPS, first, jnp.where(lane < 2 * TAPS, second, third)).astype(
        jnp.bfloat16
    )


def flat_taps(ref):
    rows = [ref[i, j].astype(jnp.float32) for i in range(3) for j in range(3)]
    return jnp.concatenate(rows, axis=0)


def prepare_kernel(
    views, edges_hbm, conv_in_hbm, conv_out_hbm, wq_hbm, wkv_hbm,
    gc, mq, mk, taps, bias, edges_ref, conv_in, conv_out, wq, wk, sems,
):
    parts = (
        (edges_hbm, edges_ref),
        (conv_in_hbm, conv_in),
        (wq_hbm, wq),
        (wkv_hbm.at[:, : HEADS * HD], wk),
        (conv_out_hbm, conv_out),
    )
    copies = [pltpu.make_async_copy(src, dst, sems.at[n]) for n, (src, dst) in enumerate(parts)]
    for copy in copies:
        copy.start()
    local = bias.shape[0]
    span = bias.shape[1]
    total = views * local
    first = lax.axis_index("view") * local
    copies[0].wait()
    source = edges_ref[0:1, :]
    target = edges_ref[1:2, :]
    slot = lax.broadcasted_iota(jnp.int32, (span, 1), 0)
    near = first - REACH + slot
    near = jnp.where(near < 0, near + total, near)
    near = jnp.where(near >= total, near - total, near)
    for v in range(local):
        own = first + v
        hit = ((source == own) & (target == near)) | ((target == own) & (source == near))
        linked = jnp.max(hit.astype(jnp.float32), axis=1, keepdims=True)
        linked = jnp.where(slot == v + REACH, 1.0, linked)
        inside = (slot >= v) & (slot <= v + 2 * REACH)
        allowed = (linked > 0.5) & inside
        bias[v] = jnp.broadcast_to(jnp.where(allowed, 0.0, NEG_FILL), bias.shape[1:])
    copies[1].wait()
    wc = flat_taps(conv_in)
    wcb = wc.astype(jnp.bfloat16)
    copies[2].wait()
    mq[...] = jnp.dot(wcb, wq[...], preferred_element_type=jnp.float32)
    copies[3].wait()
    mk[...] = jnp.dot(wcb, wk[...], preferred_element_type=jnp.float32)
    copies[4].wait()
    wt = flat_taps(conv_out)
    pad = jnp.zeros((DEEP - 3 * TAPS, wc.shape[1]), jnp.float32)
    wc3 = jnp.concatenate([wc, wc, wc, pad], axis=0).astype(jnp.bfloat16)
    taps[...] = jnp.concatenate([wc, wt], axis=0).astype(jnp.bfloat16)
    gc[...] = split_lanes(nt_dot(taps[...], wc3))


def nt_dot_parts(a, b):
    ah, bh = high(a), high(b)
    left = jnp.concatenate([ah, a - ah, ah], axis=1).astype(jnp.bfloat16)
    right = jnp.concatenate([bh, bh, b - bh], axis=1).astype(jnp.bfloat16)
    return nt_dot(left, right)


def head_pair(g):
    lane = lax.broadcasted_iota(jnp.int32, (TAPS, 2 * HD), 1)
    even = (lane < HD).astype(jnp.float32)
    return slice(g * 2 * HD, (g + 1) * 2 * HD), even, 1.0 - even


def score_products(mq, mk, aq):
    scale = math.log2(math.e) / math.sqrt(HD)
    lane = lax.broadcasted_iota(jnp.int32, (2 * TAPS, 2 * TAPS), 1)
    for g in range(HEADS // 2):
        cols, even, odd = head_pair(g)
        q = mq[:, cols] * scale
        k = mk[:, cols]
        q2 = jnp.concatenate([q, q], axis=0)
        k2 = jnp.concatenate([k * even, k * odd], axis=0)
        a = nt_dot_parts(k2, q2)
        ah = high(a)
        aq[g * 2 * TAPS : (g + 1) * 2 * TAPS, :] = jnp.where(lane < TAPS, ah, a - ah).astype(
            jnp.bfloat16
        )


def value_products(mv, nt, bb):
    for g in range(HEADS // 2):
        cols, even, odd = head_pair(g)
        v = mv[:, cols]
        v2 = jnp.concatenate([v * even, v * odd], axis=0)
        b = nt_dot_parts(nt[:, cols], v2)
        bh = high(b)
        bb[g] = jnp.concatenate([bh, b - bh], axis=0).astype(jnp.bfloat16)


def shifted(x, by):
    lane = lax.broadcasted_iota(jnp.int32, x.shape, x.ndim - 1)
    width = x.shape[-1]
    if by == 1:
        return jnp.where(lane == 0, 0.0, pltpu.roll(x, 1, x.ndim - 1))
    return jnp.where(lane == width - 1, 0.0, pltpu.roll(x, width - 1, x.ndim - 1))


def is_even(axis):
    return lax.rem(lax.axis_index(axis), 2) == 0


def pack_kernel(own, first, second, after, rows, tail, lead):
    local = own.shape[0]
    even = is_even("space")
    kind = own.dtype
    for v in range(local):
        one = first[v].astype(jnp.float32)
        two = second[v].astype(jnp.float32)
        rows[v, 0] = jnp.where(even, two, one).astype(kind)
        rows[v, 1] = own[v]
        rows[v, 2] = jnp.where(even, one, two).astype(kind)
    for n in range(REACH):
        for i in range(3):
            tail[n, i] = rows[local - REACH + n, i]
            lead[n, i] = rows[n, i]


def patch_stack(rows):
    parts = []
    for row in rows:
        row = row.astype(jnp.float32)
        parts += [shifted(row, 1), row, shifted(row, -1)]
    patch = jnp.concatenate(parts, axis=0)
    pad = jnp.zeros((DEEP - 3 * TAPS, patch.shape[1]), jnp.float32)
    return jnp.concatenate([patch, patch, patch, pad], axis=0).astype(jnp.bfloat16)


def token_rate(gram_patches, patches):
    square = jnp.sum(gram_patches * patches, axis=0, keepdims=True) * (1.0 / 1024)
    return lax.rsqrt(jnp.maximum(square, 0.0) + 1e-6)


def store_keys(keyed, slots, kl, vl):
    w = keyed.shape[1] // len(slots)
    kh = high(keyed)
    low = keyed - kh
    sub = lax.broadcasted_iota(jnp.int32, (8, w), 0)
    for n, u in enumerate(slots):
        cols = slice(n * w, (n + 1) * w)
        onehot = (sub == u).astype(jnp.float32)
        h = kh[:, cols]
        r = low[:, cols]
        vl[:, cols] = jnp.concatenate([h, jnp.ones((8, w), jnp.float32), r], axis=0).astype(
            jnp.bfloat16
        )
        tall = jnp.concatenate(
            [h, onehot, r, h, jnp.zeros((DEEP - 3 * TAPS - 8, w), jnp.float32)], axis=0
        )
        kl[cols, :] = tall.T.astype(jnp.bfloat16)


def own_kernel(
    rows, gc, mq, mk, taps, bias, wkv, wo, qr, skip, bb, top, acc, p3, aq, kl, vl, sc, ex
):
    local, _, _, w = rows.shape
    score_products(mq, mk, aq)
    mv = jnp.dot(taps[0:TAPS, :], wkv[:, HEADS * HD :], preferred_element_type=jnp.float32)
    value_products(mv, nt_dot(taps[TAPS:, :], wo[...]), bb)
    for v in range(local):
        p3[:, v * w : (v + 1) * w] = patch_stack([rows[v, i] for i in range(3)])
    base = jnp.dot(gc[...], p3[...], preferred_element_type=jnp.float32)
    asked = jnp.dot(aq[...], p3[0 : 2 * TAPS, :], preferred_element_type=jnp.float32)
    patches = p3[0:TAPS, :].astype(jnp.float32)
    rate = token_rate(base[0:TAPS], patches)
    skip[...] = base[TAPS:]
    store_keys(patches * rate, range(REACH, REACH + local), kl, vl)
    for v in range(local):
        for head in range(HEADS):
            q = asked[head * TAPS : (head + 1) * TAPS, v * w : (v + 1) * w]
            q = q * rate[:, v * w : (v + 1) * w]
            h = high(q)
            qr[v, :, head * w : (head + 1) * w] = jnp.concatenate(
                [h, bias[v], h, q - h, jnp.zeros((DEEP - 3 * TAPS - 8, w), jnp.float32)], axis=0
            ).astype(jnp.bfloat16)
    spans = [(max(v - REACH, 0) * w, min(v + REACH + 1, local) * w) for v in range(local)]

    def scored(v):
        lo, hi = spans[v]
        sc[v % 2, 0 : hi - lo, :] = jnp.dot(
            kl[lo:hi, :], qr[v], preferred_element_type=jnp.float32
        )

    scored(0)
    for v in range(local):
        if v + 1 < local:
            scored(v + 1)
        lo, hi = spans[v]
        for head in range(HEADS):
            cols = slice(head * w, (head + 1) * w)
            scores = sc[v % 2, 0 : hi - lo, cols]
            largest = jnp.max(scores, axis=0, keepdims=True)
            top[v : v + 1, cols] = largest
            ex[v % 2, 0 : hi - lo, cols] = jnp.exp2(scores - largest).astype(jnp.bfloat16)
        gathered = jnp.dot(
            vl[:, lo:hi], ex[v % 2, 0 : hi - lo, :], preferred_element_type=jnp.float32
        )
        acc[v, 0:TAPS, :] = gathered[0:TAPS] + gathered[TAPS + 8 :]
        acc[v, TAPS:, :] = gathered[TAPS : TAPS + 8]

def mix_kernel(
    prev, nxt, gc, bb, qr, skip, top, acc,
    mine, late, early, p3, kl, vl, uh, ul, sc, ex,
):
    local, _, w = mine.shape
    for u in range(REACH):
        p3[:, u * w : (u + 1) * w] = patch_stack([prev[u, i] for i in range(3)])
        p3[:, (REACH + u) * w : (REACH + u + 1) * w] = patch_stack([nxt[u, i] for i in range(3)])
    gram = jnp.dot(gc[0:TAPS, :], p3[...], preferred_element_type=jnp.float32)
    patches = p3[0:TAPS, :].astype(jnp.float32)
    rate = token_rate(gram, patches)
    slots = [*range(REACH), *range(REACH + local, 2 * REACH + local)]
    store_keys(patches * rate, slots, kl, vl)
    spans = []
    for v in range(local):
        near = [n for n, u in enumerate(slots) if v <= u <= v + 2 * REACH]
        spans.append((near[0] * w, (near[-1] + 1) * w))
    for v, (lo, hi) in enumerate(spans):
        sc[v, 0 : hi - lo, :] = jnp.dot(
            kl[lo:hi, :], qr[v], preferred_element_type=jnp.float32
        )
    for v, (lo, hi) in enumerate(spans):
        fades = []
        for head in range(HEADS):
            cols = slice(head * w, (head + 1) * w)
            scores = sc[v, 0 : hi - lo, cols]
            before = top[v : v + 1, cols]
            largest = jnp.maximum(jnp.max(scores, axis=0, keepdims=True), before)
            fades.append(jnp.exp2(before - largest))
            ex[v, 0 : hi - lo, cols] = jnp.exp2(scores - largest).astype(jnp.bfloat16)
        fade = jnp.concatenate(fades, axis=1)
        gathered = jnp.dot(
            vl[:, lo:hi], ex[v, 0 : hi - lo, :], preferred_element_type=jnp.float32
        )
        weight = gathered[TAPS : TAPS + 1] + acc[v, TAPS : TAPS + 1, :] * fade
        mixed = gathered[0:TAPS] + gathered[TAPS + 8 :] + acc[v, 0:TAPS, :] * fade
        mixed = mixed * (1.0 / weight)
        for g in range(HEADS // 2):
            pair = mixed[:, g * 2 * w : (g + 1) * 2 * w]
            pair = jnp.concatenate([pair[:, :w], pair[:, w:]], axis=0)
            h = pair.astype(jnp.bfloat16)
            uh[g, :, v * w : (v + 1) * w] = h
            ul[g, :, v * w : (v + 1) * w] = (pair - h.astype(jnp.float32)).astype(jnp.bfloat16)
    z = skip[...]
    for g in range(HEADS // 2):
        y = jnp.dot(bb[g], uh[g], preferred_element_type=jnp.float32)
        z = z + y[:TAPS] + y[TAPS:]
        z = z + jnp.dot(bb[g, 0:TAPS, :], ul[g], preferred_element_type=jnp.float32)
    even = is_even("space")
    for v in range(local):
        parts = []
        for i in range(3):
            rows = z[i * 24 : (i + 1) * 24, v * w : (v + 1) * w]
            parts.append(shifted(rows[0:8], 1) + rows[8:16] + shifted(rows[16:24], -1))
        below, mine[v], above = parts
        early[v] = jnp.where(even, below, above)
        late[v] = jnp.where(even, above, below)


def pairs(count, start):
    both = []
    for i in range(start, count - 1, 2):
        both += [(i, i + 1), (i + 1, i)]
    return both


def on_device(
    latent,
    camera_edges,
    conv_in_weight,
    query_weight,
    key_value_weight,
    out_weight,
    conv_out_weight,
):
    local, channels, _, w = latent.shape
    span = local + 2 * REACH
    views = lax.axis_size("view")
    space = lax.axis_size("space")
    x = latent.reshape(local, channels, w)
    row_first = lax.ppermute(x, "space", pairs(space, 0))
    row_second = lax.ppermute(x, "space", pairs(space, 1))

    f32, bf16 = jnp.float32, jnp.bfloat16
    whole = pl.BlockSpec(memory_space=pltpu.VMEM)
    far = pl.BlockSpec(memory_space=pltpu.HBM)
    loaded = (
        camera_edges.T,
        conv_in_weight,
        conv_out_weight,
        query_weight,
        key_value_weight,
    )
    gc, mq, mk, taps, bias = pl.pallas_call(
        functools.partial(prepare_kernel, views),
        in_specs=[far] * len(loaded),
        out_specs=[whole] * 5,
        out_shape=[
            pltpu.VMEM((2 * TAPS, DEEP), bf16),
            pltpu.VMEM((TAPS, HEADS * HD), f32),
            pltpu.VMEM((TAPS, HEADS * HD), f32),
            pltpu.VMEM((2 * TAPS, out_weight.shape[1]), bf16),
            pltpu.VMEM((local, span, w), f32),
        ],
        scratch_shapes=[
            pltpu.VMEM(a.shape, a.dtype)
            for a in (*loaded[:4], query_weight)
        ]
        + [pltpu.SemaphoreType.DMA((5,))],
        compiler_params=pltpu.CompilerParams(vmem_limit_bytes=60 * MIB),
        cost_estimate=pl.CostEstimate(
            flops=3_000_000_000, bytes_accessed=5_000_000, transcendentals=0
        ),
    )(*loaded)

    part = jax.ShapeDtypeStruct((REACH, 3, channels, w), bf16)
    rows, tail, lead = pl.pallas_call(
        pack_kernel,
        in_specs=[whole] * 3 + [pl.BlockSpec(memory_space=pl.ANY)],
        out_specs=[whole] * 3,
        out_shape=[pltpu.VMEM((local, 3, channels, w), bf16), part, part],
        compiler_params=pltpu.CompilerParams(vmem_limit_bytes=4 * MIB),
    )(x, row_first, row_second, bias)
    prev = lax.ppermute(tail, "view", [(i, (i + 1) % views) for i in range(views)])
    nxt = lax.ppermute(lead, "view", [((i + 1) % views, i) for i in range(views)])

    keys_scratch = [
        pltpu.VMEM((local * w, DEEP), bf16),
        pltpu.VMEM((2 * TAPS + 8, local * w), bf16),
    ]
    qr, skip, bb, top, acc = pl.pallas_call(
        own_kernel,
        in_specs=[whole] * 8,
        out_specs=[whole] * 5,
        out_shape=[
            pltpu.VMEM((local, DEEP, HEADS * w), bf16),
            pltpu.VMEM((TAPS, local * w), f32),
            pltpu.VMEM((HEADS // 2, 2 * TAPS, 2 * TAPS), bf16),
            pltpu.VMEM((local, HEADS * w), f32),
            pltpu.VMEM((local, TAPS + 8, HEADS * w), f32),
        ],
        scratch_shapes=[
            pltpu.VMEM((DEEP, local * w), bf16),
            pltpu.VMEM((HEADS * TAPS, 2 * TAPS), bf16),
            *keys_scratch,
            pltpu.VMEM((2, local * w, HEADS * w), f32),
            pltpu.VMEM((2, local * w, HEADS * w), bf16),
        ],
        compiler_params=pltpu.CompilerParams(vmem_limit_bytes=24 * MIB),
        cost_estimate=pl.CostEstimate(
            flops=4_000_000_000, bytes_accessed=1_000_000, transcendentals=2_000_000
        ),
    )(rows, gc, mq, mk, taps, bias, key_value_weight, out_weight)

    plane = jax.ShapeDtypeStruct((local, channels, w), f32)
    mine, late, early = pl.pallas_call(
        mix_kernel,
        in_specs=[whole] * 8,
        out_specs=[whole] * 3,
        out_shape=[plane] * 3,
        scratch_shapes=[
            pltpu.VMEM((DEEP, 2 * REACH * w), bf16),
            *keys_scratch,
            pltpu.VMEM((HEADS // 2, 2 * TAPS, local * w), bf16),
            pltpu.VMEM((HEADS // 2, 2 * TAPS, local * w), bf16),
            pltpu.VMEM((local, REACH * w, HEADS * w), f32),
            pltpu.VMEM((local, REACH * w, HEADS * w), bf16),
        ],
        compiler_params=pltpu.CompilerParams(vmem_limit_bytes=24 * MIB),
        cost_estimate=pl.CostEstimate(
            flops=3_000_000_000, bytes_accessed=1_000_000, transcendentals=1_000_000
        ),
    )(prev, nxt, gc, bb, qr, skip, top, acc)

    row_second = lax.ppermute(late, "space", pairs(space, 1))
    row_first = lax.ppermute(early, "space", pairs(space, 0))
    return (row_second + mine + row_first).reshape(local, channels, 1, w)


def solution(mesh):
    placed = (P("view", None, "space", None), P(), P(), P(), P(), P(), P())
    return jax.shard_map(
        on_device,
        mesh=mesh,
        in_specs=placed,
        out_specs=P("view", None, "space", None),
        check_vma=False,
    )
```

```python
import functools
import math

import jax
import jax.numpy as jnp
from jax import lax
from jax.experimental import pallas as pl
from jax.experimental.pallas import tpu as pltpu
from jax.sharding import PartitionSpec as P

HEADS = 8
HD = 64
REACH = 2
TAPS = 72
DEEP = 256
NEG_FILL = -1e30
MIB = 1024 * 1024


def nt_dot(a, b):
    return lax.dot_general(a, b, (((1,), (1,)), ((), ())), preferred_element_type=jnp.float32)


def high(x):
    return x.astype(jnp.bfloat16).astype(jnp.float32)


def split_lanes(x):
    lane = lax.broadcasted_iota(jnp.int32, x.shape, 1)
    first = high(x)
    rest = x - first
    second = high(rest)
    third = rest - second
    return jnp.where(lane < TAPS, first, jnp.where(lane < 2 * TAPS, second, third)).astype(
        jnp.bfloat16
    )


def flat_taps(ref):
    rows = [ref[i, j].astype(jnp.float32) for i in range(3) for j in range(3)]
    return jnp.concatenate(rows, axis=0)


def prepare_kernel(
    views, edges_hbm, conv_in_hbm, conv_out_hbm, wq_hbm, wkv_hbm,
    gc, mq, mk, taps, bias, edges_ref, conv_in, conv_out, wq, wk, sems,
):
    parts = (
        (conv_in_hbm, conv_in),
        (conv_out_hbm, conv_out),
        (edges_hbm, edges_ref),
        (wq_hbm, wq),
        (wkv_hbm.at[:, : HEADS * HD], wk),
    )
    copies = [pltpu.make_async_copy(src, dst, sems.at[n]) for n, (src, dst) in enumerate(parts)]
    for copy in copies:
        copy.start()
    copies[0].wait()
    wc = flat_taps(conv_in)
    wcb = wc.astype(jnp.bfloat16)
    copies[1].wait()
    wt = flat_taps(conv_out)
    pad = jnp.zeros((DEEP - 3 * TAPS, wc.shape[1]), jnp.float32)
    wc3 = jnp.concatenate([wc, wc, wc, pad], axis=0).astype(jnp.bfloat16)
    taps[...] = jnp.concatenate([wc, wt], axis=0).astype(jnp.bfloat16)
    gc[...] = split_lanes(nt_dot(taps[...], wc3))
    local = bias.shape[0]
    span = bias.shape[1]
    total = views * local
    first = lax.axis_index("view") * local
    copies[2].wait()
    source = edges_ref[0:1, :]
    target = edges_ref[1:2, :]
    slot = lax.broadcasted_iota(jnp.int32, (span, 1), 0)
    near = first - REACH + slot
    near = jnp.where(near < 0, near + total, near)
    near = jnp.where(near >= total, near - total, near)
    for v in range(local):
        own = first + v
        hit = ((source == own) & (target == near)) | ((target == own) & (source == near))
        linked = jnp.max(hit.astype(jnp.float32), axis=1, keepdims=True)
        linked = jnp.where(slot == v + REACH, 1.0, linked)
        inside = (slot >= v) & (slot <= v + 2 * REACH)
        allowed = (linked > 0.5) & inside
        bias[v] = jnp.broadcast_to(jnp.where(allowed, 0.0, NEG_FILL), bias.shape[1:])
    copies[3].wait()
    mq[...] = jnp.dot(wcb, wq[...], preferred_element_type=jnp.float32)
    copies[4].wait()
    mk[...] = jnp.dot(wcb, wk[...], preferred_element_type=jnp.float32)


def nt_dot_parts(a, b):
    ah, bh = high(a), high(b)
    left = jnp.concatenate([ah, a - ah, ah], axis=1).astype(jnp.bfloat16)
    right = jnp.concatenate([bh, bh, b - bh], axis=1).astype(jnp.bfloat16)
    return nt_dot(left, right)


def head_pair(g):
    lane = lax.broadcasted_iota(jnp.int32, (TAPS, 2 * HD), 1)
    even = (lane < HD).astype(jnp.float32)
    return slice(g * 2 * HD, (g + 1) * 2 * HD), even, 1.0 - even


def score_products(mq, mk, aq):
    scale = math.log2(math.e) / math.sqrt(HD)
    lane = lax.broadcasted_iota(jnp.int32, (2 * TAPS, 2 * TAPS), 1)
    for g in range(HEADS // 2):
        cols, even, odd = head_pair(g)
        q = mq[:, cols] * scale
        k = mk[:, cols]
        q2 = jnp.concatenate([q, q], axis=0)
        k2 = jnp.concatenate([k * even, k * odd], axis=0)
        a = nt_dot_parts(k2, q2)
        ah = high(a)
        aq[g * 2 * TAPS : (g + 1) * 2 * TAPS, :] = jnp.where(lane < TAPS, ah, a - ah).astype(
            jnp.bfloat16
        )


def value_products(mv, nt, bb):
    for g in range(HEADS // 2):
        cols, even, odd = head_pair(g)
        v = mv[:, cols]
        v2 = jnp.concatenate([v * even, v * odd], axis=0)
        b = nt_dot_parts(nt[:, cols], v2)
        bh = high(b)
        bb[g] = jnp.concatenate([bh, b - bh], axis=0).astype(jnp.bfloat16)


def shifted(x, by):
    lane = lax.broadcasted_iota(jnp.int32, x.shape, x.ndim - 1)
    width = x.shape[-1]
    if by == 1:
        return jnp.where(lane == 0, 0.0, pltpu.roll(x, 1, x.ndim - 1))
    return jnp.where(lane == width - 1, 0.0, pltpu.roll(x, width - 1, x.ndim - 1))


def is_even(axis):
    return lax.rem(lax.axis_index(axis), 2) == 0


def pack_kernel(own, first, second, after, rows, tail, lead):
    local = own.shape[0]
    even = is_even("space")
    kind = own.dtype
    for v in range(local):
        one = first[v].astype(jnp.float32)
        two = second[v].astype(jnp.float32)
        rows[v, 0] = jnp.where(even, two, one).astype(kind)
        rows[v, 1] = own[v]
        rows[v, 2] = jnp.where(even, one, two).astype(kind)
    for n in range(REACH):
        for i in range(3):
            tail[n, i] = rows[local - REACH + n, i]
            lead[n, i] = rows[n, i]


def patch_stack(rows):
    parts = []
    for row in rows:
        row = row.astype(jnp.float32)
        parts += [shifted(row, 1), row, shifted(row, -1)]
    patch = jnp.concatenate(parts, axis=0)
    pad = jnp.zeros((DEEP - 3 * TAPS, patch.shape[1]), jnp.float32)
    return jnp.concatenate([patch, patch, patch, pad], axis=0).astype(jnp.bfloat16)


def token_rate(gram_patches, patches):
    square = jnp.sum(gram_patches * patches, axis=0, keepdims=True) * (1.0 / 1024)
    return lax.rsqrt(jnp.maximum(square, 0.0) + 1e-6)


def store_keys(keyed, slots, kl, vl):
    w = keyed.shape[1] // len(slots)
    kh = high(keyed)
    low = keyed - kh
    sub = lax.broadcasted_iota(jnp.int32, (8, w), 0)
    for n, u in enumerate(slots):
        cols = slice(n * w, (n + 1) * w)
        onehot = (sub == u).astype(jnp.float32)
        h = kh[:, cols]
        r = low[:, cols]
        vl[:, cols] = jnp.concatenate([h, jnp.ones((8, w), jnp.float32), r], axis=0).astype(
            jnp.bfloat16
        )
        tall = jnp.concatenate(
            [h, onehot, r, h, jnp.zeros((DEEP - 3 * TAPS - 8, w), jnp.float32)], axis=0
        )
        kl[cols, :] = tall.T.astype(jnp.bfloat16)


def own_kernel(
    rows, gc, mq, mk, taps, bias, wkv, wo, qr, skip, bb, top, acc, p3, aq, kl, vl, sc, ex
):
    local, _, _, w = rows.shape
    score_products(mq, mk, aq)
    mv = jnp.dot(taps[0:TAPS, :], wkv[:, HEADS * HD :], preferred_element_type=jnp.float32)
    value_products(mv, nt_dot(taps[TAPS:, :], wo[...]), bb)
    for v in range(local):
        p3[:, v * w : (v + 1) * w] = patch_stack([rows[v, i] for i in range(3)])
    base = jnp.dot(gc[...], p3[...], preferred_element_type=jnp.float32)
    asked = jnp.dot(aq[...], p3[0 : 2 * TAPS, :], preferred_element_type=jnp.float32)
    patches = p3[0:TAPS, :].astype(jnp.float32)
    rate = token_rate(base[0:TAPS], patches)
    skip[...] = base[TAPS:]
    store_keys(patches * rate, range(REACH, REACH + local), kl, vl)
    for v in range(local):
        for head in range(HEADS):
            q = asked[head * TAPS : (head + 1) * TAPS, v * w : (v + 1) * w]
            q = q * rate[:, v * w : (v + 1) * w]
            h = high(q)
            qr[v, :, head * w : (head + 1) * w] = jnp.concatenate(
                [h, bias[v], h, q - h, jnp.zeros((DEEP - 3 * TAPS - 8, w), jnp.float32)], axis=0
            ).astype(jnp.bfloat16)
    spans = [(max(v - REACH, 0) * w, min(v + REACH + 1, local) * w) for v in range(local)]

    def scored(v):
        lo, hi = spans[v]
        sc[v % 2, 0 : hi - lo, :] = jnp.dot(
            kl[lo:hi, :], qr[v], preferred_element_type=jnp.float32
        )

    scored(0)
    for v in range(local):
        if v + 1 < local:
            scored(v + 1)
        lo, hi = spans[v]
        for head in range(HEADS):
            cols = slice(head * w, (head + 1) * w)
            scores = sc[v % 2, 0 : hi - lo, cols]
            largest = jnp.max(scores, axis=0, keepdims=True)
            top[v : v + 1, cols] = largest
            ex[v % 2, 0 : hi - lo, cols] = jnp.exp2(scores - largest).astype(jnp.bfloat16)
        gathered = jnp.dot(
            vl[:, lo:hi], ex[v % 2, 0 : hi - lo, :], preferred_element_type=jnp.float32
        )
        acc[v, 0:TAPS, :] = gathered[0:TAPS] + gathered[TAPS + 8 :]
        acc[v, TAPS:, :] = gathered[TAPS : TAPS + 8]

def mix_kernel(
    prev, nxt, gc, bb, qr, skip, top, acc,
    mine, late, early, p3, kl, vl, uh, ul, sc, ex,
):
    local, _, w = mine.shape
    for u in range(REACH):
        p3[:, u * w : (u + 1) * w] = patch_stack([prev[u, i] for i in range(3)])
        p3[:, (REACH + u) * w : (REACH + u + 1) * w] = patch_stack([nxt[u, i] for i in range(3)])
    gram = jnp.dot(gc[0:TAPS, :], p3[...], preferred_element_type=jnp.float32)
    patches = p3[0:TAPS, :].astype(jnp.float32)
    rate = token_rate(gram, patches)
    slots = [*range(REACH), *range(REACH + local, 2 * REACH + local)]
    store_keys(patches * rate, slots, kl, vl)
    spans = []
    for v in range(local):
        near = [n for n, u in enumerate(slots) if v <= u <= v + 2 * REACH]
        spans.append((near[0] * w, (near[-1] + 1) * w))
    for v, (lo, hi) in enumerate(spans):
        sc[v, 0 : hi - lo, :] = jnp.dot(
            kl[lo:hi, :], qr[v], preferred_element_type=jnp.float32
        )
    for v, (lo, hi) in enumerate(spans):
        fades = []
        for head in range(HEADS):
            cols = slice(head * w, (head + 1) * w)
            scores = sc[v, 0 : hi - lo, cols]
            before = top[v : v + 1, cols]
            largest = jnp.maximum(jnp.max(scores, axis=0, keepdims=True), before)
            fades.append(jnp.exp2(before - largest))
            ex[v, 0 : hi - lo, cols] = jnp.exp2(scores - largest).astype(jnp.bfloat16)
        fade = jnp.concatenate(fades, axis=1)
        gathered = jnp.dot(
            vl[:, lo:hi], ex[v, 0 : hi - lo, :], preferred_element_type=jnp.float32
        )
        weight = gathered[TAPS : TAPS + 1] + acc[v, TAPS : TAPS + 1, :] * fade
        mixed = gathered[0:TAPS] + gathered[TAPS + 8 :] + acc[v, 0:TAPS, :] * fade
        mixed = mixed * (1.0 / weight)
        for g in range(HEADS // 2):
            pair = mixed[:, g * 2 * w : (g + 1) * 2 * w]
            pair = jnp.concatenate([pair[:, :w], pair[:, w:]], axis=0)
            h = pair.astype(jnp.bfloat16)
            uh[g, :, v * w : (v + 1) * w] = h
            ul[g, :, v * w : (v + 1) * w] = (pair - h.astype(jnp.float32)).astype(jnp.bfloat16)
    z = skip[...]
    for g in range(HEADS // 2):
        y = jnp.dot(bb[g], uh[g], preferred_element_type=jnp.float32)
        z = z + y[:TAPS] + y[TAPS:]
        z = z + jnp.dot(bb[g, 0:TAPS, :], ul[g], preferred_element_type=jnp.float32)
    even = is_even("space")
    for v in range(local):
        parts = []
        for i in range(3):
            rows = z[i * 24 : (i + 1) * 24, v * w : (v + 1) * w]
            parts.append(shifted(rows[0:8], 1) + rows[8:16] + shifted(rows[16:24], -1))
        below, mine[v], above = parts
        early[v] = jnp.where(even, below, above)
        late[v] = jnp.where(even, above, below)


def pairs(count, start):
    both = []
    for i in range(start, count - 1, 2):
        both += [(i, i + 1), (i + 1, i)]
    return both


def on_device(
    latent,
    camera_edges,
    conv_in_weight,
    query_weight,
    key_value_weight,
    out_weight,
    conv_out_weight,
):
    local, channels, _, w = latent.shape
    span = local + 2 * REACH
    views = lax.axis_size("view")
    space = lax.axis_size("space")
    x = latent.reshape(local, channels, w)
    row_first = lax.ppermute(x, "space", pairs(space, 0))
    row_second = lax.ppermute(x, "space", pairs(space, 1))

    f32, bf16 = jnp.float32, jnp.bfloat16
    whole = pl.BlockSpec(memory_space=pltpu.VMEM)
    far = pl.BlockSpec(memory_space=pltpu.HBM)
    loaded = (
        camera_edges.T,
        conv_in_weight,
        conv_out_weight,
        query_weight,
        key_value_weight,
    )
    gc, mq, mk, taps, bias = pl.pallas_call(
        functools.partial(prepare_kernel, views),
        in_specs=[far] * len(loaded),
        out_specs=[whole] * 5,
        out_shape=[
            pltpu.VMEM((2 * TAPS, DEEP), bf16),
            pltpu.VMEM((TAPS, HEADS * HD), f32),
            pltpu.VMEM((TAPS, HEADS * HD), f32),
            pltpu.VMEM((2 * TAPS, out_weight.shape[1]), bf16),
            pltpu.VMEM((local, span, w), f32),
        ],
        scratch_shapes=[
            pltpu.VMEM(a.shape, a.dtype)
            for a in (*loaded[:4], query_weight)
        ]
        + [pltpu.SemaphoreType.DMA((5,))],
        compiler_params=pltpu.CompilerParams(vmem_limit_bytes=60 * MIB),
        cost_estimate=pl.CostEstimate(
            flops=3_000_000_000, bytes_accessed=5_000_000, transcendentals=0
        ),
    )(*loaded)

    part = jax.ShapeDtypeStruct((REACH, 3, channels, w), bf16)
    rows, tail, lead = pl.pallas_call(
        pack_kernel,
        in_specs=[whole] * 3 + [pl.BlockSpec(memory_space=pl.ANY)],
        out_specs=[whole] * 3,
        out_shape=[pltpu.VMEM((local, 3, channels, w), bf16), part, part],
        compiler_params=pltpu.CompilerParams(vmem_limit_bytes=4 * MIB),
    )(x, row_first, row_second, bias)
    prev = lax.ppermute(tail, "view", [(i, (i + 1) % views) for i in range(views)])
    nxt = lax.ppermute(lead, "view", [((i + 1) % views, i) for i in range(views)])

    keys_scratch = [
        pltpu.VMEM((local * w, DEEP), bf16),
        pltpu.VMEM((2 * TAPS + 8, local * w), bf16),
    ]
    qr, skip, bb, top, acc = pl.pallas_call(
        own_kernel,
        in_specs=[whole] * 8,
        out_specs=[whole] * 5,
        out_shape=[
            pltpu.VMEM((local, DEEP, HEADS * w), bf16),
            pltpu.VMEM((TAPS, local * w), f32),
            pltpu.VMEM((HEADS // 2, 2 * TAPS, 2 * TAPS), bf16),
            pltpu.VMEM((local, HEADS * w), f32),
            pltpu.VMEM((local, TAPS + 8, HEADS * w), f32),
        ],
        scratch_shapes=[
            pltpu.VMEM((DEEP, local * w), bf16),
            pltpu.VMEM((HEADS * TAPS, 2 * TAPS), bf16),
            *keys_scratch,
            pltpu.VMEM((2, local * w, HEADS * w), f32),
            pltpu.VMEM((2, local * w, HEADS * w), bf16),
        ],
        compiler_params=pltpu.CompilerParams(vmem_limit_bytes=24 * MIB),
        cost_estimate=pl.CostEstimate(
            flops=4_000_000_000, bytes_accessed=1_000_000, transcendentals=2_000_000
        ),
    )(rows, gc, mq, mk, taps, bias, key_value_weight, out_weight)

    plane = jax.ShapeDtypeStruct((local, channels, w), f32)
    mine, late, early = pl.pallas_call(
        mix_kernel,
        in_specs=[whole] * 8,
        out_specs=[whole] * 3,
        out_shape=[plane] * 3,
        scratch_shapes=[
            pltpu.VMEM((DEEP, 2 * REACH * w), bf16),
            *keys_scratch,
            pltpu.VMEM((HEADS // 2, 2 * TAPS, local * w), bf16),
            pltpu.VMEM((HEADS // 2, 2 * TAPS, local * w), bf16),
            pltpu.VMEM((local, REACH * w, HEADS * w), f32),
            pltpu.VMEM((local, REACH * w, HEADS * w), bf16),
        ],
        compiler_params=pltpu.CompilerParams(vmem_limit_bytes=24 * MIB),
        cost_estimate=pl.CostEstimate(
            flops=3_000_000_000, bytes_accessed=1_000_000, transcendentals=1_000_000
        ),
    )(prev, nxt, gc, bb, qr, skip, top, acc)

    row_second = lax.ppermute(late, "space", pairs(space, 1))
    row_first = lax.ppermute(early, "space", pairs(space, 0))
    return (row_second + mine + row_first).reshape(local, channels, 1, w)


def solution(mesh):
    placed = (P("view", None, "space", None), P(), P(), P(), P(), P(), P())
    return jax.shard_map(
        on_device,
        mesh=mesh,
        in_specs=placed,
        out_specs=P("view", None, "space", None),
        check_vma=False,
    )
```

```python
import functools
import math

import jax
import jax.numpy as jnp
from jax import lax
from jax.experimental import pallas as pl
from jax.experimental.pallas import tpu as pltpu
from jax.sharding import PartitionSpec as P

HEADS = 8
HD = 64
REACH = 2
TAPS = 72
DEEP = 256
NEG_FILL = -1e30
MIB = 1024 * 1024


def nt_dot(a, b):
    return lax.dot_general(a, b, (((1,), (1,)), ((), ())), preferred_element_type=jnp.float32)


def high(x):
    return x.astype(jnp.bfloat16).astype(jnp.float32)


def split_lanes(x):
    lane = lax.broadcasted_iota(jnp.int32, x.shape, 1)
    first = high(x)
    rest = x - first
    second = high(rest)
    third = rest - second
    return jnp.where(lane < TAPS, first, jnp.where(lane < 2 * TAPS, second, third)).astype(
        jnp.bfloat16
    )


def flat_taps(ref):
    rows = [ref[i, j].astype(jnp.float32) for i in range(3) for j in range(3)]
    return jnp.concatenate(rows, axis=0)


def prepare_kernel(
    views, edges_hbm, conv_in_hbm, conv_out_hbm, wq_hbm, wkv_hbm,
    gc, mq, mk, taps, bias, edges_ref, conv_in, conv_out, wqk, sems,
):
    parts = (
        (conv_in_hbm, conv_in),
        (conv_out_hbm, conv_out),
        (edges_hbm, edges_ref),
        (wq_hbm, wqk.at[:, : HEADS * HD]),
        (wkv_hbm.at[:, : HEADS * HD], wqk.at[:, HEADS * HD :]),
    )
    copies = [pltpu.make_async_copy(src, dst, sems.at[n]) for n, (src, dst) in enumerate(parts)]
    for copy in copies:
        copy.start()
    copies[0].wait()
    wc = flat_taps(conv_in)
    wcb = wc.astype(jnp.bfloat16)
    copies[1].wait()
    wt = flat_taps(conv_out)
    pad = jnp.zeros((DEEP - 3 * TAPS, wc.shape[1]), jnp.float32)
    wc3 = jnp.concatenate([wc, wc, wc, pad], axis=0).astype(jnp.bfloat16)
    taps[...] = jnp.concatenate([wc, wt], axis=0).astype(jnp.bfloat16)
    gc[...] = split_lanes(nt_dot(taps[...], wc3))
    local = bias.shape[0]
    span = bias.shape[1]
    total = views * local
    first = lax.axis_index("view") * local
    copies[2].wait()
    source = edges_ref[0:1, :]
    target = edges_ref[1:2, :]
    slot = lax.broadcasted_iota(jnp.int32, (span, 1), 0)
    near = first - REACH + slot
    near = jnp.where(near < 0, near + total, near)
    near = jnp.where(near >= total, near - total, near)
    for v in range(local):
        own = first + v
        hit = ((source == own) & (target == near)) | ((target == own) & (source == near))
        linked = jnp.max(hit.astype(jnp.float32), axis=1, keepdims=True)
        linked = jnp.where(slot == v + REACH, 1.0, linked)
        inside = (slot >= v) & (slot <= v + 2 * REACH)
        allowed = (linked > 0.5) & inside
        bias[v] = jnp.broadcast_to(jnp.where(allowed, 0.0, NEG_FILL), bias.shape[1:])
    copies[3].wait()
    copies[4].wait()
    images = jnp.dot(wcb, wqk[...], preferred_element_type=jnp.float32)
    mq[...] = images[:, : HEADS * HD]
    mk[...] = images[:, HEADS * HD :]


def nt_dot_parts(a, b):
    ah, bh = high(a), high(b)
    left = jnp.concatenate([ah, a - ah, ah], axis=1).astype(jnp.bfloat16)
    right = jnp.concatenate([bh, bh, b - bh], axis=1).astype(jnp.bfloat16)
    return nt_dot(left, right)


def head_pair(g):
    lane = lax.broadcasted_iota(jnp.int32, (TAPS, 2 * HD), 1)
    even = (lane < HD).astype(jnp.float32)
    return slice(g * 2 * HD, (g + 1) * 2 * HD), even, 1.0 - even


def score_products(mq, mk, aq):
    scale = math.log2(math.e) / math.sqrt(HD)
    lane = lax.broadcasted_iota(jnp.int32, (2 * TAPS, 2 * TAPS), 1)
    for g in range(HEADS // 2):
        cols, even, odd = head_pair(g)
        q = mq[:, cols] * scale
        k = mk[:, cols]
        q2 = jnp.concatenate([q, q], axis=0)
        k2 = jnp.concatenate([k * even, k * odd], axis=0)
        a = nt_dot_parts(k2, q2)
        ah = high(a)
        aq[g * 2 * TAPS : (g + 1) * 2 * TAPS, :] = jnp.where(lane < TAPS, ah, a - ah).astype(
            jnp.bfloat16
        )


def value_products(mv, nt, bb):
    for g in range(HEADS // 2):
        cols, even, odd = head_pair(g)
        v = mv[:, cols]
        v2 = jnp.concatenate([v * even, v * odd], axis=0)
        b = nt_dot_parts(nt[:, cols], v2)
        bh = high(b)
        bb[g] = jnp.concatenate([bh, b - bh], axis=0).astype(jnp.bfloat16)


def shifted(x, by):
    lane = lax.broadcasted_iota(jnp.int32, x.shape, x.ndim - 1)
    width = x.shape[-1]
    if by == 1:
        return jnp.where(lane == 0, 0.0, pltpu.roll(x, 1, x.ndim - 1))
    return jnp.where(lane == width - 1, 0.0, pltpu.roll(x, width - 1, x.ndim - 1))


def is_even(axis):
    return lax.rem(lax.axis_index(axis), 2) == 0


def pack_kernel(own, first, second, after, rows, tail, lead):
    local = own.shape[0]
    even = is_even("space")
    kind = own.dtype
    for v in range(local):
        one = first[v].astype(jnp.float32)
        two = second[v].astype(jnp.float32)
        rows[v, 0] = jnp.where(even, two, one).astype(kind)
        rows[v, 1] = own[v]
        rows[v, 2] = jnp.where(even, one, two).astype(kind)
    for n in range(REACH):
        for i in range(3):
            tail[n, i] = rows[local - REACH + n, i]
            lead[n, i] = rows[n, i]


def patch_stack(rows):
    parts = []
    for row in rows:
        row = row.astype(jnp.float32)
        parts += [shifted(row, 1), row, shifted(row, -1)]
    patch = jnp.concatenate(parts, axis=0)
    pad = jnp.zeros((DEEP - 3 * TAPS, patch.shape[1]), jnp.float32)
    return jnp.concatenate([patch, patch, patch, pad], axis=0).astype(jnp.bfloat16)


def token_rate(gram_patches, patches):
    square = jnp.sum(gram_patches * patches, axis=0, keepdims=True) * (1.0 / 1024)
    return lax.rsqrt(jnp.maximum(square, 0.0) + 1e-6)


def store_keys(keyed, slots, kl, vl):
    w = keyed.shape[1] // len(slots)
    kh = high(keyed)
    low = keyed - kh
    sub = lax.broadcasted_iota(jnp.int32, (8, w), 0)
    for n, u in enumerate(slots):
        cols = slice(n * w, (n + 1) * w)
        onehot = (sub == u).astype(jnp.float32)
        h = kh[:, cols]
        r = low[:, cols]
        vl[:, cols] = jnp.concatenate([h, jnp.ones((8, w), jnp.float32), r], axis=0).astype(
            jnp.bfloat16
        )
        tall = jnp.concatenate(
            [h, onehot, r, h, jnp.zeros((DEEP - 3 * TAPS - 8, w), jnp.float32)], axis=0
        )
        kl[cols, :] = tall.T.astype(jnp.bfloat16)


def own_kernel(
    rows, gc, mq, mk, taps, bias, wkv, wo, qr, skip, bb, top, acc, p3, aq, kl, vl, sc, ex
):
    local, _, _, w = rows.shape
    score_products(mq, mk, aq)
    mv = jnp.dot(taps[0:TAPS, :], wkv[:, HEADS * HD :], preferred_element_type=jnp.float32)
    value_products(mv, nt_dot(taps[TAPS:, :], wo[...]), bb)
    for v in range(local):
        p3[:, v * w : (v + 1) * w] = patch_stack([rows[v, i] for i in range(3)])
    base = jnp.dot(gc[...], p3[...], preferred_element_type=jnp.float32)
    asked = jnp.dot(aq[...], p3[0 : 2 * TAPS, :], preferred_element_type=jnp.float32)
    patches = p3[0:TAPS, :].astype(jnp.float32)
    rate = token_rate(base[0:TAPS], patches)
    skip[...] = base[TAPS:]
    store_keys(patches * rate, range(REACH, REACH + local), kl, vl)
    for v in range(local):
        for head in range(HEADS):
            q = asked[head * TAPS : (head + 1) * TAPS, v * w : (v + 1) * w]
            q = q * rate[:, v * w : (v + 1) * w]
            h = high(q)
            qr[v, :, head * w : (head + 1) * w] = jnp.concatenate(
                [h, bias[v], h, q - h, jnp.zeros((DEEP - 3 * TAPS - 8, w), jnp.float32)], axis=0
            ).astype(jnp.bfloat16)
    spans = [(max(v - REACH, 0) * w, min(v + REACH + 1, local) * w) for v in range(local)]

    def scored(v):
        lo, hi = spans[v]
        sc[v % 2, 0 : hi - lo, :] = jnp.dot(
            kl[lo:hi, :], qr[v], preferred_element_type=jnp.float32
        )

    scored(0)
    for v in range(local):
        if v + 1 < local:
            scored(v + 1)
        lo, hi = spans[v]
        for head in range(HEADS):
            cols = slice(head * w, (head + 1) * w)
            scores = sc[v % 2, 0 : hi - lo, cols]
            largest = jnp.max(scores, axis=0, keepdims=True)
            top[v : v + 1, cols] = largest
            ex[v % 2, 0 : hi - lo, cols] = jnp.exp2(scores - largest).astype(jnp.bfloat16)
        gathered = jnp.dot(
            vl[:, lo:hi], ex[v % 2, 0 : hi - lo, :], preferred_element_type=jnp.float32
        )
        acc[v, 0:TAPS, :] = gathered[0:TAPS] + gathered[TAPS + 8 :]
        acc[v, TAPS:, :] = gathered[TAPS : TAPS + 8]

def mix_kernel(
    prev, nxt, gc, bb, qr, skip, top, acc,
    mine, late, early, p3, kl, vl, uh, ul, sc, ex,
):
    local, _, w = mine.shape
    for u in range(REACH):
        p3[:, u * w : (u + 1) * w] = patch_stack([prev[u, i] for i in range(3)])
        p3[:, (REACH + u) * w : (REACH + u + 1) * w] = patch_stack([nxt[u, i] for i in range(3)])
    gram = jnp.dot(gc[0:TAPS, :], p3[...], preferred_element_type=jnp.float32)
    patches = p3[0:TAPS, :].astype(jnp.float32)
    rate = token_rate(gram, patches)
    slots = [*range(REACH), *range(REACH + local, 2 * REACH + local)]
    store_keys(patches * rate, slots, kl, vl)
    spans = []
    for v in range(local):
        near = [n for n, u in enumerate(slots) if v <= u <= v + 2 * REACH]
        spans.append((near[0] * w, (near[-1] + 1) * w))
    for v, (lo, hi) in enumerate(spans):
        sc[v, 0 : hi - lo, :] = jnp.dot(
            kl[lo:hi, :], qr[v], preferred_element_type=jnp.float32
        )
    for v, (lo, hi) in enumerate(spans):
        fades = []
        for head in range(HEADS):
            cols = slice(head * w, (head + 1) * w)
            scores = sc[v, 0 : hi - lo, cols]
            before = top[v : v + 1, cols]
            largest = jnp.maximum(jnp.max(scores, axis=0, keepdims=True), before)
            fades.append(jnp.exp2(before - largest))
            ex[v, 0 : hi - lo, cols] = jnp.exp2(scores - largest).astype(jnp.bfloat16)
        fade = jnp.concatenate(fades, axis=1)
        gathered = jnp.dot(
            vl[:, lo:hi], ex[v, 0 : hi - lo, :], preferred_element_type=jnp.float32
        )
        weight = gathered[TAPS : TAPS + 1] + acc[v, TAPS : TAPS + 1, :] * fade
        mixed = gathered[0:TAPS] + gathered[TAPS + 8 :] + acc[v, 0:TAPS, :] * fade
        mixed = mixed * (1.0 / weight)
        for g in range(HEADS // 2):
            pair = mixed[:, g * 2 * w : (g + 1) * 2 * w]
            pair = jnp.concatenate([pair[:, :w], pair[:, w:]], axis=0)
            h = pair.astype(jnp.bfloat16)
            uh[g, :, v * w : (v + 1) * w] = h
            ul[g, :, v * w : (v + 1) * w] = (pair - h.astype(jnp.float32)).astype(jnp.bfloat16)
    z = skip[...]
    for g in range(HEADS // 2):
        y = jnp.dot(bb[g], uh[g], preferred_element_type=jnp.float32)
        z = z + y[:TAPS] + y[TAPS:]
        z = z + jnp.dot(bb[g, 0:TAPS, :], ul[g], preferred_element_type=jnp.float32)
    even = is_even("space")
    for v in range(local):
        parts = []
        for i in range(3):
            rows = z[i * 24 : (i + 1) * 24, v * w : (v + 1) * w]
            parts.append(shifted(rows[0:8], 1) + rows[8:16] + shifted(rows[16:24], -1))
        below, mine[v], above = parts
        early[v] = jnp.where(even, below, above)
        late[v] = jnp.where(even, above, below)


def pairs(count, start):
    both = []
    for i in range(start, count - 1, 2):
        both += [(i, i + 1), (i + 1, i)]
    return both


def on_device(
    latent,
    camera_edges,
    conv_in_weight,
    query_weight,
    key_value_weight,
    out_weight,
    conv_out_weight,
):
    local, channels, _, w = latent.shape
    span = local + 2 * REACH
    views = lax.axis_size("view")
    space = lax.axis_size("space")
    x = latent.reshape(local, channels, w)
    row_first = lax.ppermute(x, "space", pairs(space, 0))
    row_second = lax.ppermute(x, "space", pairs(space, 1))

    f32, bf16 = jnp.float32, jnp.bfloat16
    whole = pl.BlockSpec(memory_space=pltpu.VMEM)
    far = pl.BlockSpec(memory_space=pltpu.HBM)
    loaded = (
        camera_edges.T,
        conv_in_weight,
        conv_out_weight,
        query_weight,
        key_value_weight,
    )
    gc, mq, mk, taps, bias = pl.pallas_call(
        functools.partial(prepare_kernel, views),
        in_specs=[far] * len(loaded),
        out_specs=[whole] * 5,
        out_shape=[
            pltpu.VMEM((2 * TAPS, DEEP), bf16),
            pltpu.VMEM((TAPS, HEADS * HD), f32),
            pltpu.VMEM((TAPS, HEADS * HD), f32),
            pltpu.VMEM((2 * TAPS, out_weight.shape[1]), bf16),
            pltpu.VMEM((local, span, w), f32),
        ],
        scratch_shapes=[
            pltpu.VMEM(a.shape, a.dtype)
            for a in (*loaded[:3], key_value_weight)
        ]
        + [pltpu.SemaphoreType.DMA((5,))],
        compiler_params=pltpu.CompilerParams(vmem_limit_bytes=60 * MIB),
        cost_estimate=pl.CostEstimate(
            flops=3_000_000_000, bytes_accessed=5_000_000, transcendentals=0
        ),
    )(*loaded)

    part = jax.ShapeDtypeStruct((REACH, 3, channels, w), bf16)
    rows, tail, lead = pl.pallas_call(
        pack_kernel,
        in_specs=[whole] * 3 + [pl.BlockSpec(memory_space=pl.ANY)],
        out_specs=[whole] * 3,
        out_shape=[pltpu.VMEM((local, 3, channels, w), bf16), part, part],
        compiler_params=pltpu.CompilerParams(vmem_limit_bytes=4 * MIB),
    )(x, row_first, row_second, bias)
    prev = lax.ppermute(tail, "view", [(i, (i + 1) % views) for i in range(views)])
    nxt = lax.ppermute(lead, "view", [((i + 1) % views, i) for i in range(views)])

    keys_scratch = [
        pltpu.VMEM((local * w, DEEP), bf16),
        pltpu.VMEM((2 * TAPS + 8, local * w), bf16),
    ]
    qr, skip, bb, top, acc = pl.pallas_call(
        own_kernel,
        in_specs=[whole] * 8,
        out_specs=[whole] * 5,
        out_shape=[
            pltpu.VMEM((local, DEEP, HEADS * w), bf16),
            pltpu.VMEM((TAPS, local * w), f32),
            pltpu.VMEM((HEADS // 2, 2 * TAPS, 2 * TAPS), bf16),
            pltpu.VMEM((local, HEADS * w), f32),
            pltpu.VMEM((local, TAPS + 8, HEADS * w), f32),
        ],
        scratch_shapes=[
            pltpu.VMEM((DEEP, local * w), bf16),
            pltpu.VMEM((HEADS * TAPS, 2 * TAPS), bf16),
            *keys_scratch,
            pltpu.VMEM((2, local * w, HEADS * w), f32),
            pltpu.VMEM((2, local * w, HEADS * w), bf16),
        ],
        compiler_params=pltpu.CompilerParams(vmem_limit_bytes=24 * MIB),
        cost_estimate=pl.CostEstimate(
            flops=4_000_000_000, bytes_accessed=1_000_000, transcendentals=2_000_000
        ),
    )(rows, gc, mq, mk, taps, bias, key_value_weight, out_weight)

    plane = jax.ShapeDtypeStruct((local, channels, w), f32)
    mine, late, early = pl.pallas_call(
        mix_kernel,
        in_specs=[whole] * 8,
        out_specs=[whole] * 3,
        out_shape=[plane] * 3,
        scratch_shapes=[
            pltpu.VMEM((DEEP, 2 * REACH * w), bf16),
            *keys_scratch,
            pltpu.VMEM((HEADS // 2, 2 * TAPS, local * w), bf16),
            pltpu.VMEM((HEADS // 2, 2 * TAPS, local * w), bf16),
            pltpu.VMEM((local, REACH * w, HEADS * w), f32),
            pltpu.VMEM((local, REACH * w, HEADS * w), bf16),
        ],
        compiler_params=pltpu.CompilerParams(vmem_limit_bytes=24 * MIB),
        cost_estimate=pl.CostEstimate(
            flops=3_000_000_000, bytes_accessed=1_000_000, transcendentals=1_000_000
        ),
    )(prev, nxt, gc, bb, qr, skip, top, acc)

    row_second = lax.ppermute(late, "space", pairs(space, 1))
    row_first = lax.ppermute(early, "space", pairs(space, 0))
    return (row_second + mine + row_first).reshape(local, channels, 1, w)


def solution(mesh):
    placed = (P("view", None, "space", None), P(), P(), P(), P(), P(), P())
    return jax.shard_map(
        on_device,
        mesh=mesh,
        in_specs=placed,
        out_specs=P("view", None, "space", None),
        check_vma=False,
    )
```
